512 devices in a mesh: tm: 8 (over y), tile: 64 (over x, z, core).
Axes of the slice: x: 4, y: 8, z: 8, core: 2. Of those that a mesh axis runs over, the one named last changes fastest.
Arguments:
- frames: bfloat16 [8, 64, 256, 128], P('tm', None, 'tile'), may hold values from -6 to 6
- back_shift: int32 [8, 2, 2, 256, 128], P('tm', None, None, 'tile'), may hold values from -2 to 1, as said below
- back_fraction: float32 [8, 2, 2, 256, 128], P('tm', None, None, 'tile'), may hold values from 0 to 1, as said below
- ahead_shift: int32 [8, 2, 2, 256, 128], P('tm', None, None, 'tile'), may hold values from -2 to 1, as said below
- ahead_fraction: float32 [8, 2, 2, 256, 128], P('tm', None, None, 'tile'), may hold values from 0 to 1, as said below
- back_mixer: bfloat16 [64, 192], replicated, may hold values from -0.75 to 0.75
- back_inner: bfloat16 [64, 576], replicated, may hold values from -0.25 to 0.25
- back_outer: bfloat16 [64, 576], replicated, may hold values from -0.25 to 0.25
- ahead_mixer: bfloat16 [64, 256], replicated, may hold values from -0.75 to 0.75
- ahead_inner: bfloat16 [64, 576], replicated, may hold values from -0.25 to 0.25
- ahead_outer: bfloat16 [64, 576], replicated, may hold values from -0.25 to 0.25
Outputs:
- back_features: bfloat16 [8, 64, 256, 128], P('tm', None, 'tile')
- ahead_features: bfloat16 [8, 64, 256, 128], P('tm', None, 'tile')
The draws below stay inside these ranges and needn't reach their ends.
Inputs may be any that keep to these rules, and one draw needn't show every extreme that they name: `back_shift`: row and column shifts of each sampling position. `ahead_shift`: row and column shifts of each sampling position. `back_fraction`: fractional parts of each sampling position. `ahead_fraction`: fractional parts of each sampling position.
All inputs are finite; a program needn't handle non-finite values.
Results may differ from the reference program's by a relative error of at most 0.034.
Values may be sent and summed in bfloat16 or wider, within the bound.
No kernel may reach another device: no remote copies, remote signals or barrier semaphores. Data moves between devices by JAX's collectives and lax.ppermute only.
A program may use at most 128 MiB of HBM per device.

```python
import jax
import jax.numpy as jnp
from jax import lax

C = 64
R = 2
W = 128
FRAMES = 8
H = 256


def motion_flags(key, salt_value):
    key = jax.random.fold_in(key, salt_value)
    moving = jax.random.randint(key, (FRAMES, 2), 0, 2)
    forced = jax.random.randint(jax.random.fold_in(key, 7), (), 0, FRAMES)
    frame_ids = jnp.arange(FRAMES, dtype=jnp.int32)[:, None]
    sample_ids = jnp.arange(2, dtype=jnp.int32)[None, :]
    pinned = ((frame_ids == forced) & (sample_ids == 0)).astype(jnp.int32)
    return jnp.maximum(moving, pinned)


def shift_draw(key, salt_value, own_salt):
    moving = motion_flags(key, salt_value)
    key = jax.random.fold_in(key, own_salt)
    drawn_shift = jax.random.randint(key, (FRAMES, 2, 2, H, W), 0 - R, R)
    row_part = jnp.where(moving[:, :, None, None] > 0, jnp.int32(0 - R), drawn_shift[:, :, 0])
    return jnp.stack([row_part, drawn_shift[:, :, 1]], axis=2).astype(jnp.int32)


def fraction_rows(moving, near_zero, spread_part):
    row_part = jnp.where(moving[:, :, None, None] > 0, near_zero, spread_part[:, :, 0])
    return jnp.stack([row_part, spread_part[:, :, 1]], axis=2).astype(jnp.float32)


def draw_back_shift(key, part):
    return shift_draw(key, 11, 1)


def draw_ahead_shift(key, part):
    return shift_draw(key, 12, 3)


def draw_back_fraction(key, part):
    moving = motion_flags(key, 11)
    key = jax.random.fold_in(key, 2)
    uniform_draw = jax.random.uniform(key, (FRAMES, 2, 2, H, W), jnp.float32)
    near_zero = uniform_draw[:, :, 0] ** 8
    spread_part = uniform_draw
    return fraction_rows(moving, near_zero, spread_part)


def draw_ahead_fraction(key, part):
    moving = motion_flags(key, 12)
    key = jax.random.fold_in(key, 4)
    uniform_draw = jax.random.uniform(key, (FRAMES, 2, 2, H, W), jnp.float32)
    near_zero = uniform_draw[:, :, 0] ** 8
    spread_part = uniform_draw
    return fraction_rows(moving, near_zero, spread_part)


def block_levels(rng, dims, pieces, least, largest):
    def one(dim, parts):
        heights = jax.random.uniform(jax.random.fold_in(jax.random.fold_in(rng, 6), dim), (parts,), jnp.float32, least / len(pieces), largest / len(pieces))
        return jnp.repeat(jnp.exp(heights), dims[dim] // parts).reshape((-1,) + (1,) * (len(dims) - dim - 1))

    gain = one(*pieces[0])
    for cut in pieces[1:]:
        gain = gain * one(*cut)
    return gain


def bell_draw(key, extent, scale, limit, pieces=(), kind=jnp.bfloat16):
    gain = block_levels(key, extent, pieces, -0.22, 0.18) if pieces else 1.0
    entries = jax.random.normal(key, extent, jnp.float32) * scale * gain
    return jnp.minimum(jnp.maximum(entries, -limit), limit).astype(kind)


def setup_inputs(seed: int = 0) -> dict:
    key_list = jax.random.split(jax.random.key(seed), 12)
    return {
        "frames": bell_draw(key_list[0], (FRAMES, C, H, W), 1.0, 6.0, ((0, 8), (2, 64))),
        "back_shift": draw_back_shift(jax.random.fold_in(key_list[11], 71), 0),
        "back_fraction": draw_back_fraction(jax.random.fold_in(key_list[11], 71), 0),
        "ahead_shift": draw_ahead_shift(jax.random.fold_in(key_list[11], 71), 0),
        "ahead_fraction": draw_ahead_fraction(jax.random.fold_in(key_list[11], 71), 0),
        "back_mixer": bell_draw(key_list[5], (C, 3 * C), C ** -0.5, 0.75),
        "back_inner": bell_draw(key_list[6], (C, 9 * C), (9 * C) ** -0.5, 0.25),
        "back_outer": bell_draw(key_list[7], (C, 9 * C), (9 * C) ** -0.5, 0.25),
        "ahead_mixer": bell_draw(key_list[8], (C, 4 * C), C ** -0.5, 0.75),
        "ahead_inner": bell_draw(key_list[9], (C, 9 * C), (9 * C) ** -0.5, 0.25),
        "ahead_outer": bell_draw(key_list[10], (C, 9 * C), (9 * C) ** -0.5, 0.25),
    }


def leaky(values):
    return jnp.maximum(values, 0.1 * values)


def sample(feature, shifts, fractions):
    height = shifts.shape[1]
    width = shifts.shape[2]
    source = feature.astype(jnp.float32)
    row_index = jnp.arange(height, dtype=jnp.int32)[:, None]
    col_index = jnp.arange(width, dtype=jnp.int32)[None, :]
    low_weight = lax.optimization_barrier((1.0 - fractions[1]).astype(jnp.bfloat16)).astype(jnp.float32)
    high_weight = lax.optimization_barrier(fractions[1].astype(jnp.bfloat16)).astype(jnp.float32)
    total = jnp.zeros(feature.shape, jnp.float32)
    for rise, row_weight in ((0, 1.0 - fractions[0]), (1, fractions[0])):
        partial_value = jnp.zeros(feature.shape, jnp.float32)
        for across, col_weight in ((0, low_weight), (1, high_weight)):
            rows = row_index + shifts[0] + rise
            cols = col_index + shifts[1] + across
            inside = (rows >= 0) & (rows < height) & (cols >= 0) & (cols < width)
            values = source[:, jnp.clip(rows, 0, height - 1), jnp.clip(cols, 0, width - 1)]
            partial_value = partial_value + jnp.where(inside[None], col_weight[None] * values, 0.0)
        total = total + row_weight[None] * partial_value
    return total.astype(jnp.bfloat16)


def convolve(values, kernel):
    height = values.shape[1]
    width = values.shape[2]
    padded = jnp.pad(values, ((0, 0), (1, 1), (1, 1)))
    stacked = jnp.concatenate([padded[:, above:above + height, across:across + width] for above in range(3) for across in range(3)], axis=0)
    return jnp.einsum("ok,khw->ohw", kernel.astype(jnp.float32), stacked.astype(jnp.float32))


def block(inputs, mixer, inner, outer):
    joined = leaky(jnp.einsum("ok,khw->ohw", mixer.astype(jnp.float32), inputs.astype(jnp.float32))).astype(jnp.bfloat16)
    hidden = leaky(convolve(joined, inner)).astype(jnp.bfloat16)
    return (joined.astype(jnp.float32) + convolve(hidden, outer)).astype(jnp.bfloat16)


def reference(frames, back_shift, back_fraction, ahead_shift, ahead_fraction, back_mixer, back_inner, back_outer, ahead_mixer, ahead_inner, ahead_outer):
    blank = jnp.zeros(frames.shape[1:], jnp.bfloat16)
    backward = [blank] * FRAMES
    newest = blank
    older = blank
    for frame_index in range(FRAMES - 1, -1, -1):
        first = sample(newest, back_shift[frame_index, 0], back_fraction[frame_index, 0])
        second = sample(older, back_shift[frame_index, 1], back_fraction[frame_index, 1])
        stacked = jnp.concatenate([frames[frame_index], first, second], axis=0)
        result = block(stacked, back_mixer, back_inner, back_outer)
        backward[frame_index] = result
        older = newest
        newest = result
    forward = []
    newest = blank
    older = blank
    for frame_index in range(FRAMES):
        first = sample(newest, ahead_shift[frame_index, 0], ahead_fraction[frame_index, 0])
        second = sample(older, ahead_shift[frame_index, 1], ahead_fraction[frame_index, 1])
        stacked = jnp.concatenate([frames[frame_index], backward[frame_index], first, second], axis=0)
        result = block(stacked, ahead_mixer, ahead_inner, ahead_outer)
        forward.append(result)
        older = newest
        newest = result
    return jnp.stack(backward), jnp.stack(forward)
```

```python
import functools

import jax
import jax.numpy as jnp
from jax import lax
from jax.experimental import pallas as pl
from jax.experimental.pallas import tpu as pltpu
from jax.sharding import PartitionSpec as P

R = 2
C = 64
W = 128
ROWS = 4
H = 256
FRAMES = 8
EXT = ROWS + 2 * R
ACC = jnp.bfloat16


def leaky(values):
    return jnp.maximum(values, 0.1 * values)


def tap_weights(params, row0):
    sy, sx, qy, qx = (params[n] for n in range(4))
    rows = row0 + lax.broadcasted_iota(jnp.int32, (EXT, W), 0)
    cols = lax.broadcasted_iota(jnp.int32, (EXT, W), 1)
    out = {}
    across = []
    for dx in range(-R, R + 1):
        u = jnp.where(sx == dx, 1.0 - qx, jnp.where(sx == dx - 1, qx, 0.0))
        across.append(jnp.where((cols + dx >= 0) & (cols + dx < W), u, 0.0))
    for dy in range(-R, R + 1):
        v = jnp.where(sy == dy, 1.0 - qy, jnp.where(sy == dy - 1, qy, 0.0))
        v = jnp.where((rows + dy >= 0) & (rows + dy < H), v, 0.0)
        for dx in range(-R, R + 1):
            w = v * across[dx + R]
            out[dy, dx] = pltpu.roll(w, dx % W, 1) if dx else w
    return out


def step_kernel(priors, parts, first_row, *refs):
    refs = list(refs)
    sources = [[refs.pop(0) for _ in range(3)] for _ in range(priors)]
    sides = [[refs.pop(0) for _ in range(3)] for _ in range(parts)]
    params = refs.pop(0) if priors else None
    mixer, inner, outer, out, stack, joined, hidden, wts = refs
    row0 = first_row[0] - R

    def side_row(trio, r):
        up, own, down = trio
        up_rows, down_rows = up.shape[0] // C, down.shape[0] // C
        if r < R:
            return up[pl.ds((up_rows - R + r) * C, C), :]
        if r < R + ROWS:
            return own[pl.ds((r - R) * C, C), :]
        return down[pl.ds((r - R - ROWS) * C, C), :]

    def source_row(trio, o):
        return (trio[0], (o + ROWS) * C) if o < 0 else (trio[1], o * C) if o < ROWS else (trio[2], (o - ROWS) * C)

    for p in range(priors):
        for (dy, dx), w in tap_weights(params[p], row0).items():
            wts[p * 25 + (dy + R) * 5 + dx + R] = w

    depth = (parts + priors) * C
    for r in range(EXT):
        for p in range(priors):
            taps = {}
            for dy in range(-R, R + 1):
                for dx in range(-R, R + 1):
                    w = wts[p * 25 + (dy + R) * 5 + dx + R, pl.ds(r, 1), :]
                    taps[dy, dx] = jnp.broadcast_to(w, (16, W)).astype(ACC)
            for ch in range(0, C, 16):
                g = []
                for dy in range(-R, R + 1):
                    ref, at = source_row(sources[p], r - R + dy)
                    g.append(ref[pl.ds(at + ch, 16), :].astype(ACC))
                total = None
                for dx in range(-R, R + 1):
                    t = g[0] * taps[-R, dx]
                    for dy in range(-R + 1, R + 1):
                        t = t + g[dy + R] * taps[dy, dx]
                    t = t.astype(jnp.float32)
                    t = pltpu.roll(t, -dx % W, 1) if dx else t
                    total = t if total is None else total + t
                stack[pl.ds(p * C + ch, 16), pl.ds(r * W, W)] = total.astype(jnp.bfloat16)

    for r in range(0, EXT, 2):
        pieces = [
            jnp.concatenate([side_row(trio, r), side_row(trio, r + 1)], axis=1) for trio in sides
        ]
        if priors:
            pieces.append(stack[pl.ds(0, priors * C), pl.ds(r * W, 2 * W)])
        data = jnp.concatenate(pieces, axis=0)
        both = leaky(jnp.dot(mixer[:, pl.ds(0, depth)], data, preferred_element_type=jnp.float32))
        for n in range(2):
            value = both[:, n * W : (n + 1) * W]
            if not R <= r + n < R + ROWS:
                at = row0 + r + n
                keep = jnp.where((at >= 0) & (at < H), 1.0, 0.0)
                value = value * keep
            joined[pl.ds((r + n) * C, C), :] = value.astype(jnp.bfloat16)

    cols = lax.broadcasted_iota(jnp.int32, (C, W), 1)

    def conv_pair(source, kernel, r):
        data = jnp.concatenate(
            [source[pl.ds(r * C, 3 * C), :], source[pl.ds((r + 1) * C, 3 * C), :]], axis=1
        )
        res = jnp.dot(kernel[...], data, preferred_element_type=jnp.float32)
        outs = []
        for n in range(2):
            part = res[:, n * W : (n + 1) * W]
            left = jnp.where(cols >= 1, pltpu.roll(part[0:C], 1, 1), 0.0)
            right = jnp.where(cols < W - 1, pltpu.roll(part[2 * C : 3 * C], W - 1, 1), 0.0)
            outs.append(left + part[C : 2 * C] + right)
        return outs

    for r in range(0, ROWS + 2, 2):
        for n, value in enumerate(conv_pair(joined, inner, r)):
            value = leaky(value)
            if r + n in (0, ROWS + 1):
                at = row0 + 1 + r + n
                value = value * jnp.where((at >= 0) & (at < H), 1.0, 0.0)
            hidden[pl.ds((r + n) * C, C), :] = value.astype(jnp.bfloat16)

    for r in range(0, ROWS, 2):
        for n, value in enumerate(conv_pair(hidden, outer, r)):
            base = joined[pl.ds((r + n + R) * C, C), :].astype(jnp.float32)
            out[pl.ds((r + n) * C, C), :] = (base + value).astype(jnp.bfloat16)


def run_step(first_row, sources, sides, params, weights):
    priors, parts = len(sources), len(sides)
    operands = [first_row]
    for trio in list(sources) + list(sides):
        operands += list(trio)
    if priors:
        operands.append(params)
    operands += list(weights)
    vmem = pl.BlockSpec(memory_space=pltpu.VMEM)
    specs = [pl.BlockSpec(memory_space=pltpu.SMEM)] + [vmem] * (len(operands) - 1)
    return pl.pallas_call(
        functools.partial(step_kernel, priors, parts),
        out_shape=jax.ShapeDtypeStruct((ROWS * C, W), jnp.bfloat16),
        in_specs=specs,
        out_specs=vmem,
        scratch_shapes=[
            pltpu.VMEM((2 * C, EXT * W), jnp.bfloat16),
            pltpu.VMEM((EXT * C, W), jnp.bfloat16),
            pltpu.VMEM(((ROWS + 2) * C, W), jnp.bfloat16),
            pltpu.VMEM((50, EXT, W), jnp.float32),
        ],
        compiler_params=pltpu.CompilerParams(vmem_limit_bytes=16 * 2**20),
        name="step",
    )(*operands)


def neighbours(shard):
    count = lax.axis_size("tile")
    up = lax.ppermute(shard, "tile", [(i, i + 1) for i in range(count - 1)])
    down = lax.ppermute(shard, "tile", [(i + 1, i) for i in range(count - 1)])
    return up, down


def conv_matrix(kernel):
    return kernel.reshape(C, 3, 3, C).transpose(2, 0, 1, 3).reshape(3 * C, 3 * C)


def shards(
    frames,
    back_shift,
    back_fraction,
    ahead_shift,
    ahead_fraction,
    back_mixer,
    back_inner,
    back_outer,
    ahead_mixer,
    ahead_inner,
    ahead_outer,
):
    tile = lax.axis_index("tile")
    turn = lax.axis_index("tm")
    first_row = (tile * ROWS).astype(jnp.int32).reshape(1)

    own = frames[0].transpose(1, 0, 2).reshape(ROWS * C, W)

    def pack(shift, fraction):
        return jnp.concatenate([shift[0].astype(jnp.bfloat16), fraction[0].astype(jnp.bfloat16)], axis=1)

    own_params = jnp.stack([pack(back_shift, back_fraction), pack(ahead_shift, ahead_fraction)])
    own_params = own_params.transpose(3, 0, 1, 2, 4).reshape(ROWS * 16, W)
    mine = jnp.concatenate([own, own_params], axis=0)
    clip = lax.all_gather(mine, "tm", axis=0)

    count = lax.axis_size("tile")
    low = jnp.concatenate([clip[:, 2 * C : 4 * C], clip[:, 4 * C + 32 : 4 * C + 64]], axis=1)
    high = jnp.concatenate([clip[:, 0 : 2 * C], clip[:, 4 * C : 4 * C + 32]], axis=1)
    above = lax.ppermute(low, "tile", [(i, i + 1) for i in range(count - 1)])
    below = lax.ppermute(high, "tile", [(i + 1, i) for i in range(count - 1)])
    rows = jnp.concatenate([above[:, 2 * C :], clip[:, 4 * C :], below[:, 2 * C :]], axis=1)
    params = rows.reshape(FRAMES, EXT, 2, 2, 4, W).transpose(2, 0, 3, 4, 1, 5).astype(jnp.float32)
    frame_trios = [(above[t, : 2 * C], clip[t, : 4 * C], below[t, : 2 * C]) for t in range(FRAMES)]

    def chain(order, way, extra, weights):
        done = {}
        history = []
        for n, t in enumerate(order):
            sides = [frame_trios[t]] + ([extra[t]] if extra else [])
            new = run_step(first_row, history[:2], sides, params[way, t], weights)
            if n + 1 < FRAMES or not extra:
                up, down = neighbours(new)
                history.insert(0, (up, new, down))
                done[t] = (up, new, down)
            else:
                done[t] = (None, new, None)
        return done

    back = chain(
        range(FRAMES - 1, -1, -1), 0, None, (back_mixer, conv_matrix(back_inner), conv_matrix(back_outer))
    )
    ahead = chain(
        range(FRAMES), 1, back, (ahead_mixer, conv_matrix(ahead_inner), conv_matrix(ahead_outer))
    )

    def pick(done):
        value = done[0][1]
        for t in range(1, FRAMES):
            value = jnp.where(turn == t, done[t][1], value)
        return value.reshape(ROWS, C, W).transpose(1, 0, 2)[None]

    return pick(back), pick(ahead)


def solution(mesh):
    in_specs = (
        P("tm", None, "tile", None),
        P("tm", None, None, "tile", None),
        P("tm", None, None, "tile", None),
        P("tm", None, None, "tile", None),
        P("tm", None, None, "tile", None),
        P(),
        P(),
        P(),
        P(),
        P(),
        P(),
    )
    out_specs = (P("tm", None, "tile", None), P("tm", None, "tile", None))
    return jax.shard_map(shards, mesh=mesh, in_specs=in_specs, out_specs=out_specs, check_vma=False)
```

```python
import functools

import jax
import jax.numpy as jnp
from jax import lax
from jax.experimental import pallas as pl
from jax.experimental.pallas import tpu as pltpu
from jax.sharding import PartitionSpec as P

R = 2
C = 64
W = 128
ROWS = 4
H = 256
FRAMES = 8
EXT = ROWS + 2 * R


def leaky(values):
    return jnp.maximum(values, 0.1 * values)


def tap_weights(params, grid):
    sy, sx, qy, qx = (params[n] for n in range(4))
    rows = grid[0] + grid[1] * (lax.broadcasted_iota(jnp.int32, (EXT, W), 0) - R)
    cols = lax.broadcasted_iota(jnp.int32, (EXT, W), 1)
    out = []
    across = []
    for dx in range(-R, R + 1):
        u = jnp.where(sx == dx, 1.0 - qx, jnp.where(sx == dx - 1, qx, 0.0))
        across.append(jnp.where((cols + dx >= 0) & (cols + dx < W), u, 0.0))
    for dy in range(-R, R + 1):
        v = jnp.where(sy == dy, 1.0 - qy, jnp.where(sy == dy - 1, qy, 0.0))
        at = rows + grid[1] * dy
        v = jnp.where((at >= 0) & (at < H), v, 0.0)
        for dx in range(-R, R + 1):
            w = v * across[dx + R]
            out.append(pltpu.roll(w, dx % W, 1) if dx else w)
    return out


def far_row(trio, o):
    across, own, beside = trio
    if o < 0:
        return across, (-1 - o) * C
    if o < ROWS:
        return own, o * C
    return beside, (2 * ROWS - 1 - o) * C - (ROWS * C - beside.shape[0])


def sample_row(trio, r, taps, store):
    weights = [taps(n) for n in range(25)]
    for ch in range(0, C, 16):
        g = []
        for dy in range(-R, R + 1):
            ref, at = far_row(trio, r - R + dy)
            g.append(ref[pl.ds(at + ch, 16), :])
        total = None
        for dx in range(5):
            t = g[0] * weights[dx]
            for dy in range(1, 5):
                t = t + g[dy] * weights[dy * 5 + dx]
            t = t.astype(jnp.float32)
            t = pltpu.roll(t, (R - dx) % W, 1) if dx != R else t
            total = t if total is None else total + t
        store(ch, total.astype(jnp.bfloat16))


def prepare_kernel(priors, grid, *refs):
    refs = list(refs)
    older = [refs.pop(0) for _ in range(3)] if priors == 2 else None
    params, taps = refs.pop(0), refs.pop(0)
    for n, w in enumerate(tap_weights(params[0], grid)):
        for r in range(EXT):
            taps[r, n] = jnp.broadcast_to(w[r : r + 1], (16, W)).astype(jnp.bfloat16)
    if priors < 2:
        return
    stack, wts = refs
    for n, w in enumerate(tap_weights(params[1], grid)):
        wts[n] = w
    for r in range(EXT):

        def weight(n):
            return jnp.broadcast_to(wts[n, pl.ds(r, 1), :], (16, W)).astype(jnp.bfloat16)

        def store(ch, value):
            stack[pl.ds(ch, 16), pl.ds(r * W, W)] = value

        sample_row(older, r, weight, store)


def step_kernel(priors, parts, grid, *refs):
    refs = list(refs)
    sides = [[refs.pop(0) for _ in range(3)] for _ in range(parts)]
    newest = [refs.pop(0) for _ in range(3)] if priors else None
    taps = refs.pop(0) if priors else None
    older = refs.pop(0) if priors == 2 else None
    mixer, inner, outer, out, stack, joined, hidden = refs

    def keep(row):
        at = grid[0] + grid[1] * row
        return jnp.where((at >= 0) & (at < H), 1.0, 0.0)

    def side_row(trio, r):
        ref, at = far_row(trio, r - R)
        return ref[pl.ds(at, C), :]

    depth = (parts + priors) * C
    for r in (4, 6, 2, 0):
        for n in range(2 if priors else 0):

            def store(ch, value):
                stack[pl.ds(ch, 16), pl.ds((r + n) * W, W)] = value

            sample_row(newest, r + n, lambda k: taps[r + n, k], store)
        pieces = [
            jnp.concatenate([side_row(trio, r), side_row(trio, r + 1)], axis=1) for trio in sides
        ]
        if priors:
            pieces.append(stack[:, pl.ds(r * W, 2 * W)])
        if priors == 2:
            pieces.append(older[:, pl.ds(r * W, 2 * W)])
        data = jnp.concatenate(pieces, axis=0)
        both = leaky(jnp.dot(mixer[:, pl.ds(0, depth)], data, preferred_element_type=jnp.float32))
        for n in range(2):
            value = both[:, n * W : (n + 1) * W]
            if not R <= r + n < R + ROWS:
                value = value * keep(r + n - R)
            joined[pl.ds((r + n) * C, C), :] = value.astype(jnp.bfloat16)

    cols = lax.broadcasted_iota(jnp.int32, (C, W), 1)

    def conv_pair(source, kernel, r):
        data = jnp.concatenate(
            [source[pl.ds(r * C, 3 * C), :], source[pl.ds((r + 1) * C, 3 * C), :]], axis=1
        )
        res = jnp.dot(kernel[...], data, preferred_element_type=jnp.float32)
        outs = []
        for n in range(2):
            part = res[:, n * W : (n + 1) * W]
            left = jnp.where(cols >= 1, pltpu.roll(part[0:C], 1, 1), 0.0)
            right = jnp.where(cols < W - 1, pltpu.roll(part[2 * C : 3 * C], W - 1, 1), 0.0)
            outs.append(left + part[C : 2 * C] + right)
        return outs

    for r in (4, 2, 0):
        for n, value in enumerate(conv_pair(joined, inner, r)):
            value = leaky(value)
            if r + n in (0, ROWS + 1):
                value = value * keep(r + n - 1)
            hidden[pl.ds((r + n) * C, C), :] = value.astype(jnp.bfloat16)

    for r in (2, 0):
        for n, value in enumerate(conv_pair(hidden, outer, r)):
            base = joined[pl.ds((r + n + R) * C, C), :].astype(jnp.float32)
            out[pl.ds((r + n) * C, C), :] = (base + value).astype(jnp.bfloat16)


VMEM = pl.BlockSpec(memory_space=pltpu.VMEM)
SMEM = pl.BlockSpec(memory_space=pltpu.SMEM)
BF16 = jnp.bfloat16


def run_prepare(grid, older, params):
    operands = [grid] + (list(older) if older else []) + [params]
    outs = [jax.ShapeDtypeStruct((EXT, 25, 16, W), BF16)]
    if older:
        outs.append(jax.ShapeDtypeStruct((C, EXT * W), BF16))
    return pl.pallas_call(
        functools.partial(prepare_kernel, 2 if older else 1),
        out_shape=outs,
        in_specs=[SMEM] + [VMEM] * (len(operands) - 1),
        out_specs=[VMEM] * len(outs),
        scratch_shapes=[pltpu.VMEM((25, EXT, W), jnp.float32)] if older else [],
        compiler_params=pltpu.CompilerParams(vmem_limit_bytes=16 * 2**20),
        cost_estimate=pl.CostEstimate(flops=2 * 10**7, bytes_accessed=2**20, transcendentals=0),
        name="prepare",
    )(*operands)


def run_step(grid, sides, newest, prepared, weights):
    operands = [grid]
    for trio in sides:
        operands += list(trio)
    operands += (list(newest) if newest else []) + list(prepared) + list(weights)
    return pl.pallas_call(
        functools.partial(step_kernel, len(prepared), len(sides)),
        out_shape=jax.ShapeDtypeStruct((ROWS * C, W), BF16),
        in_specs=[SMEM] + [VMEM] * (len(operands) - 1),
        out_specs=VMEM,
        scratch_shapes=[
            pltpu.VMEM((C, EXT * W), BF16),
            pltpu.VMEM((EXT * C, W), BF16),
            pltpu.VMEM(((ROWS + 2) * C, W), BF16),
        ],
        compiler_params=pltpu.CompilerParams(vmem_limit_bytes=16 * 2**20),
        cost_estimate=pl.CostEstimate(flops=10**8, bytes_accessed=2**20, transcendentals=0),
        name="step",
    )(*operands)


def swap(for_across, for_beside):
    count = lax.axis_size("tile")
    pairs = [(i, i + 1) for i in range(1, count - 1, 2)]
    across = lax.ppermute(for_across, "tile", pairs + [(j, i) for i, j in pairs])
    beside = lax.ppermute(for_beside, "tile", [(i, i ^ 1) for i in range(count)])
    return across, beside


def conv_matrix(kernel, odd):
    taps = kernel.reshape(C, 3, 3, C)
    taps = jnp.where(odd, taps[:, ::-1], taps)
    return taps.transpose(2, 0, 1, 3).reshape(3 * C, 3 * C)


def shards(
    frames,
    back_shift,
    back_fraction,
    ahead_shift,
    ahead_fraction,
    back_mixer,
    back_inner,
    back_outer,
    ahead_mixer,
    ahead_inner,
    ahead_outer,
):
    tile = lax.axis_index("tile").astype(jnp.int32)
    turn = lax.axis_index("tm")
    odd = tile % 2 == 1
    grid = jnp.stack([tile * ROWS + jnp.where(odd, ROWS - 1, 0), jnp.where(odd, -1, 1)])

    def oriented(values, axis):
        return jnp.where(odd, jnp.flip(values, axis), values)

    own = oriented(frames[0].transpose(1, 0, 2), 0).reshape(ROWS * C, W)

    def pack(shift, fraction):
        sy, sx, qy, qx = shift[0, :, 0], shift[0, :, 1], fraction[0, :, 0], fraction[0, :, 1]
        sy = jnp.where(odd, -1 - sy, sy)
        qy = jnp.where(odd, 1.0 - qy, qy)
        values = jnp.stack([v.astype(BF16) for v in (sy, sx, qy, qx)], axis=1)
        return oriented(values.transpose(2, 0, 1, 3), 0)

    own_params = jnp.stack(
        [pack(back_shift, back_fraction), pack(ahead_shift, ahead_fraction)], axis=1
    ).reshape(ROWS * 16, W)
    mine = jnp.concatenate([own, own_params], axis=0)
    clip = lax.all_to_all(
        jnp.broadcast_to(mine[None], (FRAMES,) + mine.shape), "tm", split_axis=0, concat_axis=0
    )

    top = jnp.concatenate([clip[:, : 2 * C], clip[:, 4 * C : 4 * C + 32]], axis=1)
    low = jnp.concatenate([clip[:, 2 * C : 4 * C], clip[:, 4 * C + 32 :]], axis=1)
    across, beside = swap(top, low)

    def turned(halo):
        rows = halo[:, 2 * C :].reshape(FRAMES, 2, 2, 2, 4, W)[:, ::-1].astype(jnp.float32)
        return jnp.stack([-1.0 - rows[..., 0, :], rows[..., 1, :], 1.0 - rows[..., 2, :], rows[..., 3, :]], axis=4)

    mid = clip[:, 4 * C :].reshape(FRAMES, ROWS, 2, 2, 4, W).astype(jnp.float32)
    params = jnp.concatenate([turned(across), mid, turned(beside)], axis=1).transpose(2, 0, 3, 4, 1, 5)
    frame_trios = [(across[t, : 2 * C], clip[t, : 4 * C], beside[t, : 2 * C]) for t in range(FRAMES)]

    def chain(order, way, extra, weights):
        done = {}
        history = []
        for n, t in enumerate(order):
            sides = [frame_trios[t]] + ([extra[t]] if extra else [])
            prepared = run_prepare(grid, history[1] if n > 1 else None, params[way, t]) if n else []
            new = run_step(grid, sides, history[0] if n else None, prepared, weights)
            if n + 1 < FRAMES or not extra:
                far, near = swap(new, new)
                done[t] = (far, new, near)
                history.insert(0, done[t])
            else:
                done[t] = (None, new, None)
        return done

    back_weights = (back_mixer, conv_matrix(back_inner, odd), conv_matrix(back_outer, odd))
    ahead_weights = (ahead_mixer, conv_matrix(ahead_inner, odd), conv_matrix(ahead_outer, odd))
    back = chain(range(FRAMES - 1, -1, -1), 0, None, back_weights)
    ahead = chain(range(FRAMES), 1, back, ahead_weights)

    def pick(done):
        value = done[0][1]
        for t in range(1, FRAMES):
            value = jnp.where(turn == t, done[t][1], value)
        return oriented(value.reshape(ROWS, C, W), 0).transpose(1, 0, 2)[None]

    return pick(back), pick(ahead)


def solution(mesh):
    in_specs = (
        P("tm", None, "tile", None),
        P("tm", None, None, "tile", None),
        P("tm", None, None, "tile", None),
        P("tm", None, None, "tile", None),
        P("tm", None, None, "tile", None),
        P(),
        P(),
        P(),
        P(),
        P(),
        P(),
    )
    out_specs = (P("tm", None, "tile", None), P("tm", None, "tile", None))
    return jax.shard_map(shards, mesh=mesh, in_specs=in_specs, out_specs=out_specs, check_vma=False)
```

```python
import functools

import jax
import jax.numpy as jnp
from jax import lax
from jax.experimental import pallas as pl
from jax.experimental.pallas import tpu as pltpu
from jax.sharding import PartitionSpec as P

R = 2
C = 64
W = 128
ROWS = 4
H = 256
FRAMES = 8
EXT = ROWS + 2 * R


def leaky(values):
    return jnp.maximum(values, 0.1 * values)


def tap_weights(params, grid):
    sy, sx, qy, qx = (params[n] for n in range(4))
    rows = grid[0] + grid[1] * (lax.broadcasted_iota(jnp.int32, (EXT, W), 0) - R)
    cols = lax.broadcasted_iota(jnp.int32, (EXT, W), 1)
    out = []
    across = []
    for dx in range(-R, R + 1):
        u = jnp.where(sx == dx, 1.0 - qx, jnp.where(sx == dx - 1, qx, 0.0))
        across.append(jnp.where((cols + dx >= 0) & (cols + dx < W), u, 0.0))
    for dy in range(-R, R + 1):
        v = jnp.where(sy == dy, 1.0 - qy, jnp.where(sy == dy - 1, qy, 0.0))
        at = rows + grid[1] * dy
        v = jnp.where((at >= 0) & (at < H), v, 0.0)
        for dx in range(-R, R + 1):
            w = v * across[dx + R]
            out.append(pltpu.roll(w, dx % W, 1) if dx else w)
    return out


def far_row(trio, o):
    across, own, beside = trio
    if o < 0:
        return across, (-1 - o) * C
    if o < ROWS:
        return own, o * C
    return beside, (2 * ROWS - 1 - o) * C - (ROWS * C - beside.shape[0])


def sample_row(trio, r, taps, store):
    weights = [taps(n) for n in range(25)]
    for ch in range(0, C, 16):
        g = []
        for dy in range(-R, R + 1):
            ref, at = far_row(trio, r - R + dy)
            g.append(ref[pl.ds(at + ch, 16), :])
        total = None
        for dx in range(5):
            t = g[0] * weights[dx]
            for dy in range(1, 5):
                t = t + g[dy] * weights[dy * 5 + dx]
            t = t.astype(jnp.float32)
            t = pltpu.roll(t, (R - dx) % W, 1) if dx != R else t
            total = t if total is None else total + t
        store(ch, total.astype(jnp.bfloat16))


def prepare_kernel(priors, first, sense, *refs):
    refs = list(refs)
    grid = (first[0], sense[0])
    older = [refs.pop(0) for _ in range(3)] if priors == 2 else None
    params, taps = refs.pop(0), refs.pop(0)
    for n, w in enumerate(tap_weights(params[0], grid)):
        for r in range(EXT):
            taps[r, n] = jnp.broadcast_to(w[r : r + 1], (16, W)).astype(jnp.bfloat16)
    if priors < 2:
        return
    stack, wts = refs
    for n, w in enumerate(tap_weights(params[1], grid)):
        wts[n] = w
    for r in range(EXT):

        def weight(n):
            return jnp.broadcast_to(wts[n, pl.ds(r, 1), :], (16, W)).astype(jnp.bfloat16)

        def store(ch, value):
            stack[pl.ds(ch, 16), pl.ds(r * W, W)] = value

        sample_row(older, r, weight, store)


def step_kernel(priors, parts, first, sense, *refs):
    refs = list(refs)
    grid = (first[0], sense[0])
    sides = [[refs.pop(0) for _ in range(3)] for _ in range(parts)]
    newest = [refs.pop(0) for _ in range(3)] if priors else None
    taps = refs.pop(0) if priors else None
    older = refs.pop(0) if priors == 2 else None
    mixer, inner, outer, out, stack, joined, hidden = refs

    def keep(row):
        at = grid[0] + grid[1] * row
        return jnp.where((at >= 0) & (at < H), 1.0, 0.0)

    def side_row(trio, r):
        ref, at = far_row(trio, r - R)
        return ref[pl.ds(at, C), :]

    depth = (parts + priors) * C
    for r in (4, 6, 2, 0):
        for n in range(2 if priors else 0):

            def store(ch, value):
                stack[pl.ds(ch, 16), pl.ds((r + n) * W, W)] = value

            sample_row(newest, r + n, lambda k: taps[r + n, k], store)
        pieces = [
            jnp.concatenate([side_row(trio, r), side_row(trio, r + 1)], axis=1) for trio in sides
        ]
        if priors:
            pieces.append(stack[:, pl.ds(r * W, 2 * W)])
        if priors == 2:
            pieces.append(older[:, pl.ds(r * W, 2 * W)])
        data = jnp.concatenate(pieces, axis=0)
        both = leaky(jnp.dot(mixer[:, pl.ds(0, depth)], data, preferred_element_type=jnp.float32))
        for n in range(2):
            value = both[:, n * W : (n + 1) * W]
            if not R <= r + n < R + ROWS:
                value = value * keep(r + n - R)
            joined[pl.ds((r + n) * C, C), :] = value.astype(jnp.bfloat16)

    cols = lax.broadcasted_iota(jnp.int32, (C, W), 1)

    def conv_pair(source, kernel, r):
        data = jnp.concatenate(
            [source[pl.ds(r * C, 3 * C), :], source[pl.ds((r + 1) * C, 3 * C), :]], axis=1
        )
        res = jnp.dot(kernel[...], data, preferred_element_type=jnp.float32)
        outs = []
        for n in range(2):
            part = res[:, n * W : (n + 1) * W]
            left = jnp.where(cols >= 1, pltpu.roll(part[0:C], 1, 1), 0.0)
            right = jnp.where(cols < W - 1, pltpu.roll(part[2 * C : 3 * C], W - 1, 1), 0.0)
            outs.append(left + part[C : 2 * C] + right)
        return outs

    for r in (4, 2, 0):
        for n, value in enumerate(conv_pair(joined, inner, r)):
            value = leaky(value)
            if r + n in (0, ROWS + 1):
                value = value * keep(r + n - 1)
            hidden[pl.ds((r + n) * C, C), :] = value.astype(jnp.bfloat16)

    for r in (2, 0):
        for n, value in enumerate(conv_pair(hidden, outer, r)):
            base = joined[pl.ds((r + n + R) * C, C), :].astype(jnp.float32)
            out[pl.ds((r + n) * C, C), :] = (base + value).astype(jnp.bfloat16)


VMEM = pl.BlockSpec(memory_space=pltpu.VMEM)
SMEM = pl.BlockSpec(memory_space=pltpu.SMEM)
BF16 = jnp.bfloat16


def run_prepare(grid, older, params):
    operands = list(grid) + (list(older) if older else []) + [params]
    outs = [jax.ShapeDtypeStruct((EXT, 25, 16, W), BF16)]
    if older:
        outs.append(jax.ShapeDtypeStruct((C, EXT * W), BF16))
    return pl.pallas_call(
        functools.partial(prepare_kernel, 2 if older else 1),
        out_shape=outs,
        in_specs=[SMEM, SMEM] + [VMEM] * (len(operands) - 2),
        out_specs=[VMEM] * len(outs),
        scratch_shapes=[pltpu.VMEM((25, EXT, W), jnp.float32)] if older else [],
        compiler_params=pltpu.CompilerParams(vmem_limit_bytes=16 * 2**20),
        cost_estimate=pl.CostEstimate(flops=2 * 10**7, bytes_accessed=2**20, transcendentals=0),
        name="prepare",
    )(*operands)


def run_step(grid, sides, newest, prepared, weights):
    operands = list(grid)
    for trio in sides:
        operands += list(trio)
    operands += (list(newest) if newest else []) + list(prepared) + list(weights)
    return pl.pallas_call(
        functools.partial(step_kernel, len(prepared), len(sides)),
        out_shape=jax.ShapeDtypeStruct((ROWS * C, W), BF16),
        in_specs=[SMEM, SMEM] + [VMEM] * (len(operands) - 2),
        out_specs=VMEM,
        scratch_shapes=[
            pltpu.VMEM((C, EXT * W), BF16),
            pltpu.VMEM((EXT * C, W), BF16),
            pltpu.VMEM(((ROWS + 2) * C, W), BF16),
        ],
        compiler_params=pltpu.CompilerParams(vmem_limit_bytes=16 * 2**20),
        cost_estimate=pl.CostEstimate(flops=10**8, bytes_accessed=2**20, transcendentals=0),
        name="step",
    )(*operands)


def place(replica, low, p, count):
    x, z, core = p // 16, p // 2 % 8, p % 2
    half = z // 4
    level = 7 - z if half else z
    level = level if low else 7 - level
    return (2 * replica + half) * count + x * 16 + level * 2 + core


def mirror(q):
    return q // 16 * 16 + (7 - q // 2 % 8) * 2 + q % 2


def swap(for_across, for_beside):
    count = lax.axis_size("tile")
    across, beside = [], []
    for replica in range(4):
        for low in (True, False):
            at = [place(replica, low, p, count) for p in range(count)]
            for p in range(count):
                beside.append((at[p], at[p ^ 1]))
                other = p + 1 if p % 2 else p - 1
                if 0 <= other < count:
                    across.append((at[p], at[other]))
    axes = ("tm", "tile")
    return lax.ppermute(for_across, axes, across), lax.ppermute(for_beside, axes, beside)


def conv_matrix(kernel, odd):
    taps = kernel.reshape(C, 3, 3, C)
    taps = jnp.where(odd, taps[:, ::-1], taps)
    return taps.transpose(2, 0, 1, 3).reshape(3 * C, 3 * C)


def shards(
    frames,
    back_shift,
    back_fraction,
    ahead_shift,
    ahead_fraction,
    back_mixer,
    back_inner,
    back_outer,
    ahead_mixer,
    ahead_inner,
    ahead_outer,
):
    where = lax.axis_index("tile").astype(jnp.int32)
    turn = lax.axis_index("tm").astype(jnp.int32)
    odd = where % 2 == 1
    upper = where // 2 % 8 >= 4
    home = upper == (turn % 2 == 1)
    tile = jnp.where(home, where, mirror(where))
    grid = (
        (tile * ROWS + jnp.where(odd, ROWS - 1, 0)).reshape(1),
        jnp.where(odd, -1, 1).astype(jnp.int32).reshape(1),
    )

    def oriented(values, axis):
        return jnp.where(odd, jnp.flip(values, axis), values)

    own = oriented(frames[0].transpose(1, 0, 2), 0).reshape(ROWS * C, W)

    def pack(shift, fraction):
        sy, sx, qy, qx = shift[0, :, 0], shift[0, :, 1], fraction[0, :, 0], fraction[0, :, 1]
        sy = jnp.where(odd, -1 - sy, sy)
        qy = jnp.where(odd, 1.0 - qy, qy)
        values = jnp.stack([v.astype(BF16) for v in (sy, sx, qy, qx)], axis=1)
        return oriented(values.transpose(2, 0, 1, 3), 0)

    own_params = jnp.stack(
        [pack(back_shift, back_fraction), pack(ahead_shift, ahead_fraction)], axis=1
    ).reshape(ROWS * 16, W)
    mine = jnp.concatenate([own, own_params], axis=0)
    other = lax.ppermute(mine, "tile", [(q, mirror(q)) for q in range(lax.axis_size("tile"))])
    for_even = jnp.where(upper, other, mine)
    for_odd = jnp.where(upper, mine, other)
    clip = lax.all_to_all(
        jnp.stack([for_even, for_odd] * (FRAMES // 2)), "tm", split_axis=0, concat_axis=0
    )

    top = jnp.concatenate([clip[:, : 2 * C], clip[:, 4 * C : 4 * C + 32]], axis=1)
    low = jnp.concatenate([clip[:, 2 * C : 4 * C], clip[:, 4 * C + 32 :]], axis=1)
    across, beside = swap(top, low)

    def turned(halo):
        rows = halo[:, 2 * C :].reshape(FRAMES, 2, 2, 2, 4, W)[:, ::-1].astype(jnp.float32)
        return jnp.stack([-1.0 - rows[..., 0, :], rows[..., 1, :], 1.0 - rows[..., 2, :], rows[..., 3, :]], axis=4)

    mid = clip[:, 4 * C :].reshape(FRAMES, ROWS, 2, 2, 4, W).astype(jnp.float32)
    params = jnp.concatenate([turned(across), mid, turned(beside)], axis=1).transpose(2, 0, 3, 4, 1, 5)
    frame_trios = [(across[t, : 2 * C], clip[t, : 4 * C], beside[t, : 2 * C]) for t in range(FRAMES)]

    def chain(order, way, extra, weights):
        done = {}
        history = []
        for n, t in enumerate(order):
            sides = [frame_trios[t]] + ([extra[t]] if extra else [])
            prepared = run_prepare(grid, history[1] if n > 1 else None, params[way, t]) if n else []
            new = run_step(grid, sides, history[0] if n else None, prepared, weights)
            if n + 1 < FRAMES or not extra:
                far, near = swap(new, new)
                done[t] = (far, new, near)
                history.insert(0, done[t])
            else:
                done[t] = (None, new, None)
        return done

    back_weights = (back_mixer, conv_matrix(back_inner, odd), conv_matrix(back_outer, odd))
    ahead_weights = (ahead_mixer, conv_matrix(ahead_inner, odd), conv_matrix(ahead_outer, odd))
    back = chain(range(FRAMES - 1, -1, -1), 0, None, back_weights)
    ahead = chain(range(FRAMES), 1, back, ahead_weights)

    def pick(done, frame):
        value = done[0][1]
        for t in range(1, FRAMES):
            value = jnp.where(frame == t, done[t][1], value)
        return value

    def results(frame):
        return jnp.stack([pick(back, frame), pick(ahead, frame)])

    count = lax.axis_size("tile")
    gives = [
        (t * count + q, (t ^ 1) * count + q)
        for t in range(FRAMES)
        for q in range(count)
        if (q // 2 % 8 >= 4) == (t % 2 == 1)
    ]
    given = lax.ppermute(results(turn ^ 1), ("tm", "tile"), gives)
    final = jnp.where(home, results(turn), given).reshape(2, ROWS, C, W)
    final = oriented(final, 1).transpose(0, 2, 1, 3)
    return final[0][None], final[1][None]


def solution(mesh):
    in_specs = (
        P("tm", None, "tile", None),
        P("tm", None, None, "tile", None),
        P("tm", None, None, "tile", None),
        P("tm", None, None, "tile", None),
        P("tm", None, None, "tile", None),
        P(),
        P(),
        P(),
        P(),
        P(),
        P(),
    )
    out_specs = (P("tm", None, "tile", None), P("tm", None, "tile", None))
    return jax.shard_map(shards, mesh=mesh, in_specs=in_specs, out_specs=out_specs, check_vma=False)
```

```python
import functools

import jax
import jax.numpy as jnp
from jax import lax
from jax.experimental import pallas as pl
from jax.experimental.pallas import tpu as pltpu
from jax.sharding import PartitionSpec as P

R = 2
C = 64
W = 128
ROWS = 4
H = 256
FRAMES = 8
EXT = ROWS + 2 * R
EARLY = EXT // 2


def leaky(values):
    return jnp.maximum(values, 0.1 * values)


def tap_weights(params, grid):
    sy, sx, qy, qx = (params[n] for n in range(4))
    rows = grid[0] + grid[1] * (lax.broadcasted_iota(jnp.int32, (EXT, W), 0) - R)
    cols = lax.broadcasted_iota(jnp.int32, (EXT, W), 1)
    out = []
    across = []
    for dx in range(-R, R + 1):
        u = jnp.where(sx == dx, 1.0 - qx, jnp.where(sx == dx - 1, qx, 0.0))
        across.append(jnp.where((cols + dx >= 0) & (cols + dx < W), u, 0.0))
    for dy in range(-R, R + 1):
        v = jnp.where(sy == dy, 1.0 - qy, jnp.where(sy == dy - 1, qy, 0.0))
        at = rows + grid[1] * dy
        v = jnp.where((at >= 0) & (at < H), v, 0.0)
        for dx in range(-R, R + 1):
            w = v * across[dx + R]
            out.append(pltpu.roll(w, dx % W, 1) if dx else w)
    return out


def far_row(trio, o):
    across, own, beside = trio
    if o < 0:
        return across, (-1 - o) * C
    if o < ROWS:
        return own, o * C
    return beside, (2 * ROWS - 1 - o) * C - (ROWS * C - beside.shape[0])


def sample_row(trio, r, taps, store):
    weights = [taps(n) for n in range(25)]
    for ch in range(0, C, 16):
        g = []
        for dy in range(-R, R + 1):
            ref, at = far_row(trio, r - R + dy)
            g.append(ref[pl.ds(at + ch, 16), :])
        total = None
        for dx in range(5):
            t = g[0] * weights[dx]
            for dy in range(1, 5):
                t = t + g[dy] * weights[dy * 5 + dx]
            t = t.astype(jnp.float32)
            t = pltpu.roll(t, (R - dx) % W, 1) if dx != R else t
            total = t if total is None else total + t
        store(ch, total.astype(jnp.bfloat16))


def prepare_kernel(priors, first, sense, *refs):
    refs = list(refs)
    grid = (first[0], sense[0])
    newest = [refs.pop(0) for _ in range(2)] + [None]
    older = [refs.pop(0) for _ in range(3)] if priors == 2 else None
    params, taps, early = refs.pop(0), refs.pop(0), refs.pop(0)
    stack = refs.pop(0) if priors == 2 else None
    wts = refs.pop(0)

    for p in range(priors):
        for n, w in enumerate(tap_weights(params[p], grid)):
            wts[p * 25 + n] = w

    def weight(p, r, n):
        return jnp.broadcast_to(wts[p * 25 + n, pl.ds(r, 1), :], (16, W)).astype(jnp.bfloat16)

    for r in range(EARLY):

        def store_early(ch, value):
            early[pl.ds(ch, 16), pl.ds(r * W, W)] = value

        sample_row(newest, r, lambda n: weight(0, r, n), store_early)
    for r in range(EARLY, EXT):
        for n in range(25):
            taps[r - EARLY, n] = weight(0, r, n)
    for r in range(EXT if older else 0):

        def store(ch, value):
            stack[pl.ds(ch, 16), pl.ds(r * W, W)] = value

        sample_row(older, r, lambda n: weight(1, r, n), store)


def step_kernel(priors, parts, first, sense, *refs):
    refs = list(refs)
    grid = (first[0], sense[0])
    sides = [[refs.pop(0) for _ in range(3)] for _ in range(parts)]
    newest = [refs.pop(0) for _ in range(3)] if priors else None
    taps = refs.pop(0) if priors else None
    early = refs.pop(0) if priors else None
    older = refs.pop(0) if priors == 2 else None
    mixer, inner, outer, out, stack, joined, hidden = refs

    def keep(row):
        at = grid[0] + grid[1] * row
        return jnp.where((at >= 0) & (at < H), 1.0, 0.0)

    def side_row(trio, r):
        ref, at = far_row(trio, r - R)
        return ref[pl.ds(at, C), :]

    depth = (parts + priors) * C
    for r in range(0, EXT, 2):
        for n in range(2 if priors and r >= EARLY else 0):

            def store(ch, value):
                stack[pl.ds(ch, 16), pl.ds((r + n - EARLY) * W, W)] = value

            sample_row(newest, r + n, lambda k: taps[r + n - EARLY, k], store)
        pieces = [
            jnp.concatenate([side_row(trio, r), side_row(trio, r + 1)], axis=1) for trio in sides
        ]
        if priors:
            near = early[:, pl.ds(r * W, 2 * W)] if r < EARLY else stack[:, pl.ds((r - EARLY) * W, 2 * W)]
            pieces.append(near)
        if priors == 2:
            pieces.append(older[:, pl.ds(r * W, 2 * W)])
        data = jnp.concatenate(pieces, axis=0)
        both = leaky(jnp.dot(mixer[:, pl.ds(0, depth)], data, preferred_element_type=jnp.float32))
        for n in range(2):
            value = both[:, n * W : (n + 1) * W]
            if not R <= r + n < R + ROWS:
                value = value * keep(r + n - R)
            joined[pl.ds((r + n) * C, C), :] = value.astype(jnp.bfloat16)

    cols = lax.broadcasted_iota(jnp.int32, (C, W), 1)

    def conv_pair(source, kernel, r):
        data = jnp.concatenate(
            [source[pl.ds(r * C, 3 * C), :], source[pl.ds((r + 1) * C, 3 * C), :]], axis=1
        )
        res = jnp.dot(kernel[...], data, preferred_element_type=jnp.float32)
        outs = []
        for n in range(2):
            part = res[:, n * W : (n + 1) * W]
            left = jnp.where(cols >= 1, pltpu.roll(part[0:C], 1, 1), 0.0)
            right = jnp.where(cols < W - 1, pltpu.roll(part[2 * C : 3 * C], W - 1, 1), 0.0)
            outs.append(left + part[C : 2 * C] + right)
        return outs

    for r in (0, 2, 4):
        for n, value in enumerate(conv_pair(joined, inner, r)):
            value = leaky(value)
            if r + n in (0, ROWS + 1):
                value = value * keep(r + n - 1)
            hidden[pl.ds((r + n) * C, C), :] = value.astype(jnp.bfloat16)

    for r in (0, 2):
        for n, value in enumerate(conv_pair(hidden, outer, r)):
            base = joined[pl.ds((r + n + R) * C, C), :].astype(jnp.float32)
            out[pl.ds((r + n) * C, C), :] = (base + value).astype(jnp.bfloat16)


VMEM = pl.BlockSpec(memory_space=pltpu.VMEM)
SMEM = pl.BlockSpec(memory_space=pltpu.SMEM)
BF16 = jnp.bfloat16


def run_prepare(grid, newest, older, params):
    operands = list(grid) + list(newest[:2]) + (list(older) if older else []) + [params]
    outs = [
        jax.ShapeDtypeStruct((EXT - EARLY, 25, 16, W), BF16),
        jax.ShapeDtypeStruct((C, EARLY * W), BF16),
    ]
    if older:
        outs.append(jax.ShapeDtypeStruct((C, EXT * W), BF16))
    return pl.pallas_call(
        functools.partial(prepare_kernel, 2 if older else 1),
        out_shape=outs,
        in_specs=[SMEM, SMEM] + [VMEM] * (len(operands) - 2),
        out_specs=[VMEM] * len(outs),
        scratch_shapes=[pltpu.VMEM((50, EXT, W), jnp.float32)],
        compiler_params=pltpu.CompilerParams(vmem_limit_bytes=16 * 2**20),
        cost_estimate=pl.CostEstimate(flops=2 * 10**7, bytes_accessed=2**20, transcendentals=0),
        name="prepare",
    )(*operands)


def run_step(grid, sides, newest, prepared, weights):
    operands = list(grid)
    for trio in sides:
        operands += list(trio)
    operands += (list(newest) if newest else []) + list(prepared) + list(weights)
    return pl.pallas_call(
        functools.partial(step_kernel, max(0, len(prepared) - 1), len(sides)),
        out_shape=jax.ShapeDtypeStruct((ROWS * C, W), BF16),
        in_specs=[SMEM, SMEM] + [VMEM] * (len(operands) - 2),
        out_specs=VMEM,
        scratch_shapes=[
            pltpu.VMEM((C, (EXT - EARLY) * W), BF16),
            pltpu.VMEM((EXT * C, W), BF16),
            pltpu.VMEM(((ROWS + 2) * C, W), BF16),
        ],
        compiler_params=pltpu.CompilerParams(vmem_limit_bytes=16 * 2**20),
        cost_estimate=pl.CostEstimate(flops=10**8, bytes_accessed=2**20, transcendentals=0),
        name="step",
    )(*operands)


def swap(for_across, for_beside):
    count = lax.axis_size("tile")
    pairs = [(i, i + 1) for i in range(1, count - 1, 2)]
    across = lax.ppermute(for_across, "tile", pairs + [(j, i) for i, j in pairs])
    beside = lax.ppermute(for_beside, "tile", [(i, i ^ 1) for i in range(count)])
    return across, beside


def conv_matrix(kernel, odd):
    taps = kernel.reshape(C, 3, 3, C)
    taps = jnp.where(odd, taps[:, ::-1], taps)
    return taps.transpose(2, 0, 1, 3).reshape(3 * C, 3 * C)


def shards(
    frames,
    back_shift,
    back_fraction,
    ahead_shift,
    ahead_fraction,
    back_mixer,
    back_inner,
    back_outer,
    ahead_mixer,
    ahead_inner,
    ahead_outer,
):
    tile = lax.axis_index("tile").astype(jnp.int32)
    turn = lax.axis_index("tm")
    odd = tile % 2 == 1
    grid = (
        (tile * ROWS + jnp.where(odd, ROWS - 1, 0)).reshape(1),
        jnp.where(odd, -1, 1).astype(jnp.int32).reshape(1),
    )

    def oriented(values, axis):
        return jnp.where(odd, jnp.flip(values, axis), values)

    own = oriented(frames[0].transpose(1, 0, 2), 0).reshape(ROWS * C, W)

    def pack(shift, fraction):
        sy, sx, qy, qx = shift[0, :, 0], shift[0, :, 1], fraction[0, :, 0], fraction[0, :, 1]
        sy = jnp.where(odd, -1 - sy, sy)
        qy = jnp.where(odd, 1.0 - qy, qy)
        values = jnp.stack([v.astype(BF16) for v in (sy, sx, qy, qx)], axis=1)
        return oriented(values.transpose(2, 0, 1, 3), 0)

    own_params = jnp.stack(
        [pack(back_shift, back_fraction), pack(ahead_shift, ahead_fraction)], axis=1
    ).reshape(ROWS * 16, W)
    mine = jnp.concatenate([own, own_params], axis=0)
    clip = lax.all_to_all(
        jnp.broadcast_to(mine[None], (FRAMES,) + mine.shape), "tm", split_axis=0, concat_axis=0
    )

    top = jnp.concatenate([clip[:, : 2 * C], clip[:, 4 * C : 4 * C + 32]], axis=1)
    low = jnp.concatenate([clip[:, 2 * C : 4 * C], clip[:, 4 * C + 32 :]], axis=1)
    across, beside = swap(top, low)

    def turned(halo):
        rows = halo[:, 2 * C :].reshape(FRAMES, 2, 2, 2, 4, W)[:, ::-1].astype(jnp.float32)
        return jnp.stack([-1.0 - rows[..., 0, :], rows[..., 1, :], 1.0 - rows[..., 2, :], rows[..., 3, :]], axis=4)

    mid = clip[:, 4 * C :].reshape(FRAMES, ROWS, 2, 2, 4, W).astype(jnp.float32)
    params = jnp.concatenate([turned(across), mid, turned(beside)], axis=1).transpose(2, 0, 3, 4, 1, 5)
    frame_trios = [(across[t, : 2 * C], clip[t, : 4 * C], beside[t, : 2 * C]) for t in range(FRAMES)]

    def chain(order, way, extra, weights):
        done = {}
        history = []
        for n, t in enumerate(order):
            sides = [frame_trios[t]] + ([extra[t]] if extra else [])
            prepared = []
            if n:
                prepared = run_prepare(grid, history[0], history[1] if n > 1 else None, params[way, t])
            new = run_step(grid, sides, history[0] if n else None, prepared, weights)
            if n + 1 < FRAMES or not extra:
                far, near = swap(new, new)
                done[t] = (far, new, near)
                history.insert(0, done[t])
            else:
                done[t] = (None, new, None)
        return done

    back_weights = (back_mixer, conv_matrix(back_inner, odd), conv_matrix(back_outer, odd))
    ahead_weights = (ahead_mixer, conv_matrix(ahead_inner, odd), conv_matrix(ahead_outer, odd))
    back = chain(range(FRAMES - 1, -1, -1), 0, None, back_weights)
    ahead = chain(range(FRAMES), 1, back, ahead_weights)

    def pick(done):
        value = done[0][1]
        for t in range(1, FRAMES):
            value = jnp.where(turn == t, done[t][1], value)
        return oriented(value.reshape(ROWS, C, W), 0).transpose(1, 0, 2)[None]

    return pick(back), pick(ahead)


def solution(mesh):
    in_specs = (
        P("tm", None, "tile", None),
        P("tm", None, None, "tile", None),
        P("tm", None, None, "tile", None),
        P("tm", None, None, "tile", None),
        P("tm", None, None, "tile", None),
        P(),
        P(),
        P(),
        P(),
        P(),
        P(),
    )
    out_specs = (P("tm", None, "tile", None), P("tm", None, "tile", None))
    return jax.shard_map(shards, mesh=mesh, in_specs=in_specs, out_specs=out_specs, check_vma=False)
```

```python
import functools

import jax
import jax.numpy as jnp
from jax import lax
from jax.experimental import pallas as pl
from jax.experimental.pallas import tpu as pltpu
from jax.sharding import PartitionSpec as P

R = 2
C = 64
W = 128
ROWS = 4
H = 256
FRAMES = 8
EXT = ROWS + 2 * R
EARLY = EXT // 2


def leaky(values):
    return jnp.maximum(values, 0.1 * values)


def tap_weights(params, grid):
    sy, sx, qy, qx = (params[n] for n in range(4))
    rows = grid[0] + grid[1] * (lax.broadcasted_iota(jnp.int32, (EXT, W), 0) - R)
    cols = lax.broadcasted_iota(jnp.int32, (EXT, W), 1)
    out = []
    across = []
    for dx in range(-R, R + 1):
        u = jnp.where(sx == dx, 1.0 - qx, jnp.where(sx == dx - 1, qx, 0.0))
        across.append(jnp.where((cols + dx >= 0) & (cols + dx < W), u, 0.0))
    for dy in range(-R, R + 1):
        v = jnp.where(sy == dy, 1.0 - qy, jnp.where(sy == dy - 1, qy, 0.0))
        at = rows + grid[1] * dy
        v = jnp.where((at >= 0) & (at < H), v, 0.0)
        for dx in range(-R, R + 1):
            w = v * across[dx + R]
            out.append(pltpu.roll(w, dx % W, 1) if dx else w)
    return out


def far_row(trio, o):
    across, own, beside = trio
    if o < 0:
        return across, (-1 - o) * C
    if o < ROWS:
        return own, o * C
    return beside, (2 * ROWS - 1 - o) * C - (ROWS * C - beside.shape[0])


def sample_row(trio, r, taps, store):
    weights = [taps(n) for n in range(25)]
    for ch in range(0, C, 16):
        g = []
        for dy in range(-R, R + 1):
            ref, at = far_row(trio, r - R + dy)
            g.append(ref[pl.ds(at + ch, 16), :])
        total = None
        for dx in range(5):
            t = g[0] * weights[dx]
            for dy in range(1, 5):
                t = t + g[dy] * weights[dy * 5 + dx]
            t = pltpu.roll(t, (R - dx) % W, 1) if dx != R else t
            total = t if total is None else total + t
        store(ch, total)


def prepare_kernel(priors, first, sense, *refs):
    refs = list(refs)
    grid = (first[0], sense[0])
    older = [refs.pop(0) for _ in range(3)] if priors == 2 else None
    params, taps = refs.pop(0), refs.pop(0)
    for n, w in enumerate(tap_weights(params[0], grid)):
        for r in range(EXT):
            taps[r, n] = jnp.broadcast_to(w[r : r + 1], (16, W)).astype(jnp.bfloat16)
    if priors < 2:
        return
    stack, wts = refs
    for n, w in enumerate(tap_weights(params[1], grid)):
        wts[n] = w
    for r in range(EXT):

        def weight(n):
            return jnp.broadcast_to(wts[n, pl.ds(r, 1), :], (16, W)).astype(jnp.bfloat16)

        def store(ch, value):
            stack[pl.ds(ch, 16), pl.ds(r * W, W)] = value

        sample_row(older, r, weight, store)


def middle_kernel(own, beside, taps, stack):
    for r in range(EARLY, EXT):

        def store(ch, value):
            stack[pl.ds(ch, 16), pl.ds((r - EARLY) * W, W)] = value

        sample_row((None, own, beside), r, lambda n: taps[r, n], store)


def step_kernel(priors, parts, first, sense, *refs):
    refs = list(refs)
    grid = (first[0], sense[0])
    sides = [[refs.pop(0) for _ in range(3)] for _ in range(parts)]
    newest = [refs.pop(0) for _ in range(2)] + [None] if priors else None
    taps = refs.pop(0) if priors else None
    middle = refs.pop(0) if priors else None
    older = refs.pop(0) if priors == 2 else None
    mixer, inner, outer, out, stack, joined, hidden = refs

    def keep(row):
        at = grid[0] + grid[1] * row
        return jnp.where((at >= 0) & (at < H), 1.0, 0.0)

    def side_row(trio, r):
        ref, at = far_row(trio, r - R)
        return ref[pl.ds(at, C), :]

    depth = (parts + priors) * C
    for r in (0, 2, 4, 6):
        for n in range(2 if priors and r < EARLY else 0):

            def store(ch, value):
                stack[pl.ds(ch, 16), pl.ds((r + n) * W, W)] = value

            sample_row(newest, r + n, lambda k: taps[r + n, k], store)
        pieces = [
            jnp.concatenate([side_row(trio, r), side_row(trio, r + 1)], axis=1) for trio in sides
        ]
        if priors:
            near = stack[:, pl.ds(r * W, 2 * W)] if r < EARLY else middle[:, pl.ds((r - EARLY) * W, 2 * W)]
            pieces.append(near)
        if priors == 2:
            pieces.append(older[:, pl.ds(r * W, 2 * W)])
        data = jnp.concatenate(pieces, axis=0)
        both = leaky(jnp.dot(mixer[:, pl.ds(0, depth)], data, preferred_element_type=jnp.float32))
        for n in range(2):
            value = both[:, n * W : (n + 1) * W]
            if not R <= r + n < R + ROWS:
                value = value * keep(r + n - R)
            joined[pl.ds((r + n) * C, C), :] = value.astype(jnp.bfloat16)

    cols = lax.broadcasted_iota(jnp.int32, (C, W), 1)

    def conv_pair(source, kernel, r):
        data = jnp.concatenate(
            [source[pl.ds(r * C, 3 * C), :], source[pl.ds((r + 1) * C, 3 * C), :]], axis=1
        )
        res = jnp.dot(kernel[...], data, preferred_element_type=jnp.float32)
        outs = []
        for n in range(2):
            part = res[:, n * W : (n + 1) * W]
            left = jnp.where(cols >= 1, pltpu.roll(part[0:C], 1, 1), 0.0)
            right = jnp.where(cols < W - 1, pltpu.roll(part[2 * C : 3 * C], W - 1, 1), 0.0)
            outs.append(left + part[C : 2 * C] + right)
        return outs

    for r in (0, 2, 4):
        for n, value in enumerate(conv_pair(joined, inner, r)):
            value = leaky(value)
            if r + n in (0, ROWS + 1):
                value = value * keep(r + n - 1)
            hidden[pl.ds((r + n) * C, C), :] = value.astype(jnp.bfloat16)

    for r in (0, 2):
        for n, value in enumerate(conv_pair(hidden, outer, r)):
            base = joined[pl.ds((r + n + R) * C, C), :].astype(jnp.float32)
            out[pl.ds((r + n) * C, C), :] = (base + value).astype(jnp.bfloat16)


VMEM = pl.BlockSpec(memory_space=pltpu.VMEM)
SMEM = pl.BlockSpec(memory_space=pltpu.SMEM)
BF16 = jnp.bfloat16


def run_prepare(grid, older, params):
    operands = list(grid) + (list(older) if older else []) + [params]
    outs = [jax.ShapeDtypeStruct((EXT, 25, 16, W), BF16)]
    if older:
        outs.append(jax.ShapeDtypeStruct((C, EXT * W), BF16))
    return pl.pallas_call(
        functools.partial(prepare_kernel, 2 if older else 1),
        out_shape=outs,
        in_specs=[SMEM, SMEM] + [VMEM] * (len(operands) - 2),
        out_specs=[VMEM] * len(outs),
        scratch_shapes=[pltpu.VMEM((25, EXT, W), jnp.float32)] if older else [],
        compiler_params=pltpu.CompilerParams(vmem_limit_bytes=16 * 2**20),
        cost_estimate=pl.CostEstimate(flops=10**10, bytes_accessed=2**20, transcendentals=0),
        name="prepare",
    )(*operands)


def run_middle(newest, taps):
    return pl.pallas_call(
        middle_kernel,
        out_shape=jax.ShapeDtypeStruct((C, (EXT - EARLY) * W), BF16),
        in_specs=[VMEM] * 3,
        out_specs=VMEM,
        compiler_params=pltpu.CompilerParams(vmem_limit_bytes=16 * 2**20),
        cost_estimate=pl.CostEstimate(flops=10**6, bytes_accessed=2**10, transcendentals=0),
        name="middle",
    )(newest[1], newest[2], taps)


def run_step(grid, sides, newest, prepared, weights):
    operands = list(grid)
    for trio in sides:
        operands += list(trio)
    operands += (list(newest[:2]) if newest else []) + list(prepared) + list(weights)
    return pl.pallas_call(
        functools.partial(step_kernel, max(0, len(prepared) - 1), len(sides)),
        out_shape=jax.ShapeDtypeStruct((ROWS * C, W), BF16),
        in_specs=[SMEM, SMEM] + [VMEM] * (len(operands) - 2),
        out_specs=VMEM,
        scratch_shapes=[
            pltpu.VMEM((C, EARLY * W), BF16),
            pltpu.VMEM((EXT * C, W), BF16),
            pltpu.VMEM(((ROWS + 2) * C, W), BF16),
        ],
        compiler_params=pltpu.CompilerParams(vmem_limit_bytes=16 * 2**20),
        cost_estimate=pl.CostEstimate(flops=10**8, bytes_accessed=2**20, transcendentals=0),
        name="step",
    )(*operands)


def place(replica, low, p, count):
    x, z, core = p // 16, p // 2 % 8, p % 2
    half = z // 4
    level = 7 - z if half else z
    level = level if low else 7 - level
    return (2 * replica + half) * count + x * 16 + level * 2 + core


def mirror(q):
    return q // 16 * 16 + (7 - q // 2 % 8) * 2 + q % 2


def swap(for_across, for_beside):
    count = lax.axis_size("tile")
    across, beside = [], []
    for replica in range(4):
        for low in (True, False):
            at = [place(replica, low, p, count) for p in range(count)]
            for p in range(count):
                beside.append((at[p], at[p ^ 1]))
                other = p + 1 if p % 2 else p - 1
                if 0 <= other < count:
                    across.append((at[p], at[other]))
    axes = ("tm", "tile")
    return lax.ppermute(for_across, axes, across), lax.ppermute(for_beside, axes, beside)


def conv_matrix(kernel, odd):
    taps = kernel.reshape(C, 3, 3, C)
    taps = jnp.where(odd, taps[:, ::-1], taps)
    return taps.transpose(2, 0, 1, 3).reshape(3 * C, 3 * C)


def shards(
    frames,
    back_shift,
    back_fraction,
    ahead_shift,
    ahead_fraction,
    back_mixer,
    back_inner,
    back_outer,
    ahead_mixer,
    ahead_inner,
    ahead_outer,
):
    where = lax.axis_index("tile").astype(jnp.int32)
    turn = lax.axis_index("tm").astype(jnp.int32)
    odd = where % 2 == 1
    upper = where // 2 % 8 >= 4
    home = upper == (turn % 2 == 1)
    tile = jnp.where(home, where, mirror(where))
    grid = (
        (tile * ROWS + jnp.where(odd, ROWS - 1, 0)).reshape(1),
        jnp.where(odd, -1, 1).astype(jnp.int32).reshape(1),
    )

    def oriented(values, axis):
        return jnp.where(odd, jnp.flip(values, axis), values)

    own = oriented(frames[0].transpose(1, 0, 2), 0).reshape(ROWS * C, W)

    raw = jnp.concatenate(
        [
            jnp.concatenate([back_shift.astype(jnp.float32), back_fraction], axis=2),
            jnp.concatenate([ahead_shift.astype(jnp.float32), ahead_fraction], axis=2),
        ]
    )
    first = jnp.where(odd, -1.0 - raw[:, :, 0:1], raw[:, :, 0:1])
    third = jnp.where(odd, 1.0 - raw[:, :, 2:3], raw[:, :, 2:3])
    raw = jnp.concatenate([first, raw[:, :, 1:2], third, raw[:, :, 3:4]], axis=2).astype(BF16)
    own_params = oriented(raw.transpose(3, 0, 1, 2, 4), 0).reshape(ROWS * 16, W)
    mine = jnp.concatenate([own, own_params], axis=0)
    other = lax.ppermute(mine, "tile", [(q, mirror(q)) for q in range(lax.axis_size("tile"))])
    for_even = jnp.where(upper, other, mine)
    for_odd = jnp.where(upper, mine, other)
    clip = lax.all_to_all(
        jnp.broadcast_to(jnp.stack([for_even, for_odd])[None], (FRAMES // 2, 2) + mine.shape).reshape(
            (FRAMES,) + mine.shape
        ),
        "tm",
        split_axis=0,
        concat_axis=0,
    )

    top = jnp.concatenate([clip[:, : 2 * C], clip[:, 4 * C : 4 * C + 32]], axis=1)
    low = jnp.concatenate([clip[:, 2 * C : 4 * C], clip[:, 4 * C + 32 :]], axis=1)
    across, beside = swap(top, low)

    def turned(halo):
        rows = halo[:, 2 * C :].reshape(FRAMES, 2, 2, 2, 4, W)[:, ::-1].astype(jnp.float32)
        return jnp.stack([-1.0 - rows[..., 0, :], rows[..., 1, :], 1.0 - rows[..., 2, :], rows[..., 3, :]], axis=4)

    mid = clip[:, 4 * C :].reshape(FRAMES, ROWS, 2, 2, 4, W).astype(jnp.float32)
    params = jnp.concatenate([turned(across), mid, turned(beside)], axis=1).transpose(2, 0, 3, 4, 1, 5)
    frame_trios = [(across[t, : 2 * C], clip[t, : 4 * C], beside[t, : 2 * C]) for t in range(FRAMES)]

    def chain(order, way, extra, weights):
        done = {}
        history = []
        for n, t in enumerate(order):
            sides = [frame_trios[t]] + ([extra[t]] if extra else [])
            prepared = []
            if n:
                taps, *older = run_prepare(grid, history[1] if n > 1 else None, params[way, t])
                prepared = [taps, run_middle(history[0], taps)] + older
            new = run_step(grid, sides, history[0] if n else None, prepared, weights)
            if n + 1 < FRAMES or not extra:
                far, near = swap(new, new)
                done[t] = (far, new, near)
                history.insert(0, done[t])
            else:
                done[t] = (None, new, None)
        return done

    back_weights = (back_mixer, conv_matrix(back_inner, odd), conv_matrix(back_outer, odd))
    ahead_weights = (ahead_mixer, conv_matrix(ahead_inner, odd), conv_matrix(ahead_outer, odd))
    back = chain(range(FRAMES - 1, -1, -1), 0, None, back_weights)
    ahead = chain(range(FRAMES), 1, back, ahead_weights)

    def pick(done, frame):
        value = done[0][1]
        for t in range(1, FRAMES):
            value = jnp.where(frame == t, done[t][1], value)
        return value

    def results(frame):
        return jnp.stack([pick(back, frame), pick(ahead, frame)])

    count = lax.axis_size("tile")
    gives = [
        (t * count + q, (t ^ 1) * count + q)
        for t in range(FRAMES)
        for q in range(count)
        if (q // 2 % 8 >= 4) == (t % 2 == 1)
    ]
    given = lax.ppermute(results(turn ^ 1), ("tm", "tile"), gives)
    final = jnp.where(home, results(turn), given).reshape(2, ROWS, C, W)
    final = oriented(final, 1).transpose(0, 2, 1, 3)
    return final[0][None], final[1][None]


def solution(mesh):
    in_specs = (
        P("tm", None, "tile", None),
        P("tm", None, None, "tile", None),
        P("tm", None, None, "tile", None),
        P("tm", None, None, "tile", None),
        P("tm", None, None, "tile", None),
        P(),
        P(),
        P(),
        P(),
        P(),
        P(),
    )
    out_specs = (P("tm", None, "tile", None), P("tm", None, "tile", None))
    return jax.shard_map(shards, mesh=mesh, in_specs=in_specs, out_specs=out_specs, check_vma=False)
```

```python
import functools

import jax
import jax.numpy as jnp
from jax import lax
from jax.experimental import pallas as pl
from jax.experimental.pallas import tpu as pltpu
from jax.sharding import PartitionSpec as P

R = 2
C = 64
W = 128
ROWS = 4
H = 256
FRAMES = 8
EXT = ROWS + 2 * R
EARLY = EXT // 2


VMEM = pl.BlockSpec(memory_space=pltpu.VMEM)
SMEM = pl.BlockSpec(memory_space=pltpu.SMEM)
BF16 = jnp.bfloat16


def leaky(values):
    return jnp.maximum(values, 0.1 * values)


def tap_weights(params, grid):
    sy, sx, qy, qx = (params[n] for n in range(4))
    rows = grid[0] + grid[1] * (lax.broadcasted_iota(jnp.int32, (EXT, W), 0) - R)
    cols = lax.broadcasted_iota(jnp.int32, (EXT, W), 1)
    out = []
    across = []
    for dx in range(-R, R + 1):
        u = jnp.where(sx == dx, 1.0 - qx, jnp.where(sx == dx - 1, qx, 0.0))
        across.append(jnp.where((cols + dx >= 0) & (cols + dx < W), u, 0.0))
    for dy in range(-R, R + 1):
        v = jnp.where(sy == dy, 1.0 - qy, jnp.where(sy == dy - 1, qy, 0.0))
        at = rows + grid[1] * dy
        v = jnp.where((at >= 0) & (at < H), v, 0.0)
        for dx in range(-R, R + 1):
            w = v * across[dx + R]
            out.append(pltpu.roll(w, dx % W, 1) if dx else w)
    return out


def far_row(trio, o):
    across, own, beside = trio
    if o < 0:
        return across, (-1 - o) * C
    if o < ROWS:
        return own, o * C
    return beside, (2 * ROWS - 1 - o) * C - (ROWS * C - beside.shape[0])


def sample_row(trio, r, taps, store):
    weights = [taps(n) for n in range(25)]
    for ch in range(0, C, 16):
        g = []
        for dy in range(-R, R + 1):
            ref, at = far_row(trio, r - R + dy)
            g.append(ref[pl.ds(at + ch, 16), :])
        total = None
        for dx in range(5):
            t = g[0] * weights[dx]
            for dy in range(1, 5):
                t = t + g[dy] * weights[dy * 5 + dx]
            t = pltpu.roll(t, (R - dx) % W, 1) if dx != R else t
            total = t if total is None else total + t
        store(ch, total)


def prepare_kernel(priors, first, sense, *refs):
    refs = list(refs)
    grid = (first[0], sense[0])
    older = [refs.pop(0) for _ in range(3)] if priors == 2 else None
    params, taps = refs.pop(0), refs.pop(0)
    for n, w in enumerate(tap_weights(params[0], grid)):
        for r in range(EXT):
            taps[r, n] = jnp.broadcast_to(w[r : r + 1], (16, W)).astype(jnp.bfloat16)
    if priors < 2:
        return
    stack, wts = refs
    for n, w in enumerate(tap_weights(params[1], grid)):
        wts[n] = w
    for r in range(EXT):

        def weight(n):
            return jnp.broadcast_to(wts[n, pl.ds(r, 1), :], (16, W)).astype(jnp.bfloat16)

        def store(ch, value):
            stack[pl.ds(ch, 16), pl.ds(r * W, W)] = value

        sample_row(older, r, weight, store)


def middle_kernel(own, beside, taps, stack):
    for r in range(EARLY, EXT):

        def store(ch, value):
            stack[pl.ds(ch, 16), pl.ds((r - EARLY) * W, W)] = value

        sample_row((None, own, beside), r, lambda n: taps[r, n], store)


def step_kernel(priors, parts, wide, first, sense, *refs):
    refs = list(refs)
    grid = (first[0], sense[0])
    sides = [[refs.pop(0) for _ in range(3)] for _ in range(parts)]
    newest = [refs.pop(0) for _ in range(2)] + [None] if priors else None
    taps = refs.pop(0) if priors else None
    middle = refs.pop(0) if priors else None
    older = refs.pop(0) if priors == 2 else None
    mixer, inner, outer, out, stack, joined, hidden = refs

    def keep(row):
        at = grid[0] + grid[1] * row
        return jnp.where((at >= 0) & (at < H), 1.0, 0.0)

    def side_row(trio, r):
        ref, at = far_row(trio, r - R)
        return ref[pl.ds(at, C), :]

    depth = (parts + priors) * C
    cols = lax.broadcasted_iota(jnp.int32, (C, W), 1)
    span = 3 * C if wide else C
    own = C if wide else 0

    def put(ref, row, value):
        value = value.astype(BF16)
        ref[pl.ds(row * span + own, C), :] = value
        if wide:
            ref[pl.ds(row * span, C), :] = pltpu.roll(value, 1, 1) * (cols >= 1).astype(BF16)
            ref[pl.ds(row * span + 2 * C, C), :] = pltpu.roll(value, W - 1, 1) * (cols < W - 1).astype(BF16)

    def conv_pair(source, kernel, r):
        data = jnp.concatenate(
            [source[pl.ds(n * span, 3 * span), :] for n in (r, r + 1)], axis=1
        )
        res = jnp.dot(kernel[...], data, preferred_element_type=jnp.float32)
        outs = []
        for n in range(2):
            part = res[:, n * W : (n + 1) * W]
            if not wide:
                left = jnp.where(cols >= 1, pltpu.roll(part[0:C], 1, 1), 0.0)
                right = jnp.where(cols < W - 1, pltpu.roll(part[2 * C : 3 * C], W - 1, 1), 0.0)
                part = left + part[C : 2 * C] + right
            outs.append(part)
        return outs

    def join(r):
        pieces = [
            jnp.concatenate([side_row(trio, r), side_row(trio, r + 1)], axis=1) for trio in sides
        ]
        if priors:
            near = stack[:, pl.ds(r * W, 2 * W)] if r < EARLY else middle[:, pl.ds((r - EARLY) * W, 2 * W)]
            pieces.append(near)
        if priors == 2:
            pieces.append(older[:, pl.ds(r * W, 2 * W)])
        data = jnp.concatenate(pieces, axis=0)
        both = leaky(jnp.dot(mixer[:, pl.ds(0, depth)], data, preferred_element_type=jnp.float32))
        for n in range(2):
            value = both[:, n * W : (n + 1) * W]
            if not R <= r + n < R + ROWS:
                value = value * keep(r + n - R)
            put(joined, r + n, value)

    def inside(r):
        for n, value in enumerate(conv_pair(joined, inner, r)):
            value = leaky(value)
            if r + n in (0, ROWS + 1):
                value = value * keep(r + n - 1)
            put(hidden, r + n, value)

    join(4)
    join(6)
    inside(4)
    for r in (2, 0):
        for n in (1, 0) if priors else ():

            def store(ch, value):
                stack[pl.ds(ch, 16), pl.ds((r + n) * W, W)] = value

            sample_row(newest, r + n, lambda k: taps[r + n, k], store)
        join(r)
        inside(r)
    for r in (2, 0):
        for n, value in enumerate(conv_pair(hidden, outer, r)):
            base = joined[pl.ds((r + n + R) * span + own, C), :].astype(jnp.float32)
            out[pl.ds((r + n) * C, C), :] = (base + value).astype(BF16)


def pack_kernel(sense, back_shift, back_fraction, ahead_shift, ahead_fraction, out):
    turned = sense[0] < 0
    sign = jnp.where(turned, -1.0, 1.0)
    one = jnp.where(turned, 1.0, 0.0)
    for r in range(ROWS):
        row = pl.ds(jnp.where(turned, ROWS - 1 - r, r), 1)
        rows = []
        for shift, fraction in ((back_shift, back_fraction), (ahead_shift, ahead_fraction)):
            for n in range(2):
                rows.append(shift[0, n, 0, row, :].astype(jnp.float32) * sign - one)
                rows.append(shift[0, n, 1, row, :].astype(jnp.float32))
                rows.append(fraction[0, n, 0, row, :] * sign + one)
                rows.append(fraction[0, n, 1, row, :])
        out[pl.ds(r * 16, 16), :] = jnp.concatenate(rows, axis=0).astype(BF16)


def run_prepare(grid, older, params):
    operands = list(grid) + (list(older) if older else []) + [params]
    outs = [jax.ShapeDtypeStruct((EXT, 25, 16, W), BF16)]
    if older:
        outs.append(jax.ShapeDtypeStruct((C, EXT * W), BF16))
    return pl.pallas_call(
        functools.partial(prepare_kernel, 2 if older else 1),
        out_shape=outs,
        in_specs=[SMEM, SMEM] + [VMEM] * (len(operands) - 2),
        out_specs=[VMEM] * len(outs),
        scratch_shapes=[pltpu.VMEM((25, EXT, W), jnp.float32)] if older else [],
        compiler_params=pltpu.CompilerParams(vmem_limit_bytes=16 * 2**20),
        cost_estimate=pl.CostEstimate(flops=10**10, bytes_accessed=2**20, transcendentals=0),
        name="prepare",
    )(*operands)


def run_middle(newest, taps):
    return pl.pallas_call(
        middle_kernel,
        out_shape=jax.ShapeDtypeStruct((C, (EXT - EARLY) * W), BF16),
        in_specs=[VMEM] * 3,
        out_specs=VMEM,
        compiler_params=pltpu.CompilerParams(vmem_limit_bytes=16 * 2**20),
        cost_estimate=pl.CostEstimate(flops=10**6, bytes_accessed=2**10, transcendentals=0),
        name="middle",
    )(newest[1], newest[2], taps)


def run_pack(grid, arrays):
    return pl.pallas_call(
        pack_kernel,
        out_shape=jax.ShapeDtypeStruct((ROWS * 16, W), BF16),
        in_specs=[SMEM] + [VMEM] * 4,
        out_specs=VMEM,
        compiler_params=pltpu.CompilerParams(vmem_limit_bytes=16 * 2**20),
        name="pack",
    )(grid[1], *arrays)


def run_step(grid, sides, newest, prepared, weights, wide):
    operands = list(grid)
    for trio in sides:
        operands += list(trio)
    operands += (list(newest[:2]) if newest else []) + list(prepared) + list(weights)
    return pl.pallas_call(
        functools.partial(step_kernel, max(0, len(prepared) - 1), len(sides), wide),
        out_shape=jax.ShapeDtypeStruct((ROWS * C, W), BF16),
        in_specs=[SMEM, SMEM] + [VMEM] * (len(operands) - 2),
        out_specs=VMEM,
        scratch_shapes=[
            pltpu.VMEM((C, EARLY * W), BF16),
            pltpu.VMEM((EXT * C * (3 if wide else 1), W), BF16),
            pltpu.VMEM(((ROWS + 2) * C * (3 if wide else 1), W), BF16),
        ],
        compiler_params=pltpu.CompilerParams(vmem_limit_bytes=16 * 2**20),
        cost_estimate=pl.CostEstimate(flops=10**8, bytes_accessed=2**20, transcendentals=0),
        name="step",
    )(*operands)


def place(replica, low, p, count):
    x, z, core = p // 16, p // 2 % 8, p % 2
    half = z // 4
    level = 7 - z if half else z
    level = level if low else 7 - level
    return (2 * replica + half) * count + x * 16 + level * 2 + core


def mirror(q):
    return q // 16 * 16 + (7 - q // 2 % 8) * 2 + q % 2


def swap(for_across, for_beside):
    count = lax.axis_size("tile")
    across, beside = [], []
    for replica in range(4):
        for low in (True, False):
            at = [place(replica, low, p, count) for p in range(count)]
            for p in range(count):
                beside.append((at[p], at[p ^ 1]))
                other = p + 1 if p % 2 else p - 1
                if 0 <= other < count:
                    across.append((at[p], at[other]))
    axes = ("tm", "tile")
    return lax.ppermute(for_across, axes, across), lax.ppermute(for_beside, axes, beside)


def conv_matrix(kernel, odd, wide):
    taps = kernel.reshape(C, 3, 3, C)
    taps = jnp.where(odd, taps[:, ::-1], taps)
    if wide:
        return taps.reshape(C, 9 * C)
    return taps.transpose(2, 0, 1, 3).reshape(3 * C, 3 * C)


def shards(
    frames,
    back_shift,
    back_fraction,
    ahead_shift,
    ahead_fraction,
    back_mixer,
    back_inner,
    back_outer,
    ahead_mixer,
    ahead_inner,
    ahead_outer,
):
    where = lax.axis_index("tile").astype(jnp.int32)
    turn = lax.axis_index("tm").astype(jnp.int32)
    odd = where % 2 == 1
    upper = where // 2 % 8 >= 4
    home = upper == (turn % 2 == 1)
    tile = jnp.where(home, where, mirror(where))
    grid = (
        (tile * ROWS + jnp.where(odd, ROWS - 1, 0)).reshape(1),
        jnp.where(odd, -1, 1).astype(jnp.int32).reshape(1),
    )

    def oriented(values, axis):
        return jnp.where(odd, jnp.flip(values, axis), values)

    own = oriented(frames[0].transpose(1, 0, 2), 0).reshape(ROWS * C, W)

    own_params = run_pack(grid, (back_shift, back_fraction, ahead_shift, ahead_fraction))
    mine = jnp.concatenate([own, own_params], axis=0)
    other = lax.ppermute(mine, "tile", [(q, mirror(q)) for q in range(lax.axis_size("tile"))])
    for_even = jnp.where(upper, other, mine)
    for_odd = jnp.where(upper, mine, other)
    clip = lax.all_to_all(
        jnp.broadcast_to(jnp.stack([for_even, for_odd])[None], (FRAMES // 2, 2) + mine.shape).reshape(
            (FRAMES,) + mine.shape
        ),
        "tm",
        split_axis=0,
        concat_axis=0,
    )

    top = jnp.concatenate([clip[:, : 2 * C], clip[:, 4 * C : 4 * C + 32]], axis=1)
    low = jnp.concatenate([clip[:, 2 * C : 4 * C], clip[:, 4 * C + 32 :]], axis=1)
    across, beside = swap(top, low)

    def turned(halo):
        rows = halo[:, 2 * C :].reshape(FRAMES, 2, 2, 2, 4, W)[:, ::-1].astype(jnp.float32)
        return jnp.stack([-1.0 - rows[..., 0, :], rows[..., 1, :], 1.0 - rows[..., 2, :], rows[..., 3, :]], axis=4)

    mid = clip[:, 4 * C :].reshape(FRAMES, ROWS, 2, 2, 4, W).astype(jnp.float32)
    params = jnp.concatenate([turned(across), mid, turned(beside)], axis=1).transpose(2, 0, 3, 4, 1, 5)
    frame_trios = [(across[t, : 2 * C], clip[t, : 4 * C], beside[t, : 2 * C]) for t in range(FRAMES)]

    def chain(order, way, extra, weights):
        done = {}
        history = []
        for n, t in enumerate(order):
            sides = [frame_trios[t]] + ([extra[t]] if extra else [])
            prepared = []
            if n:
                taps, *older = run_prepare(grid, history[1] if n > 1 else None, params[way, t])
                prepared = [taps, run_middle(history[0], taps)] + older
            new = run_step(grid, sides, history[0] if n else None, prepared, weights, bool(extra))
            if n + 1 < FRAMES or not extra:
                far, near = swap(new, new)
                done[t] = (far, new, near)
                history.insert(0, done[t])
            else:
                done[t] = (None, new, None)
        return done

    back_weights = (back_mixer, conv_matrix(back_inner, odd, False), conv_matrix(back_outer, odd, False))
    ahead_weights = (ahead_mixer, conv_matrix(ahead_inner, odd, True), conv_matrix(ahead_outer, odd, True))
    back = chain(range(FRAMES - 1, -1, -1), 0, None, back_weights)
    ahead = chain(range(FRAMES), 1, back, ahead_weights)

    def pick(done, frame):
        value = done[0][1]
        for t in range(1, FRAMES):
            value = jnp.where(frame == t, done[t][1], value)
        return value

    def results(frame):
        return jnp.stack([pick(back, frame), pick(ahead, frame)])

    count = lax.axis_size("tile")
    gives = [
        (t * count + q, (t ^ 1) * count + q)
        for t in range(FRAMES)
        for q in range(count)
        if (q // 2 % 8 >= 4) == (t % 2 == 1)
    ]
    given = lax.ppermute(results(turn ^ 1), ("tm", "tile"), gives)
    final = jnp.where(home, results(turn), given).reshape(2, ROWS, C, W)
    final = oriented(final, 1).transpose(0, 2, 1, 3)
    return final[0][None], final[1][None]


def solution(mesh):
    in_specs = (
        P("tm", None, "tile", None),
        P("tm", None, None, "tile", None),
        P("tm", None, None, "tile", None),
        P("tm", None, None, "tile", None),
        P("tm", None, None, "tile", None),
        P(),
        P(),
        P(),
        P(),
        P(),
        P(),
    )
    out_specs = (P("tm", None, "tile", None), P("tm", None, "tile", None))
    return jax.shard_map(shards, mesh=mesh, in_specs=in_specs, out_specs=out_specs, check_vma=False)
```

```python
import functools

import jax
import jax.numpy as jnp
from jax import lax
from jax.experimental import pallas as pl
from jax.experimental.pallas import tpu as pltpu
from jax.sharding import PartitionSpec as P

R = 2
C = 64
W = 128
ROWS = 4
H = 256
FRAMES = 8
EXT = ROWS + 2 * R
EARLY = EXT // 2


VMEM = pl.BlockSpec(memory_space=pltpu.VMEM)
SMEM = pl.BlockSpec(memory_space=pltpu.SMEM)
BF16 = jnp.bfloat16


def leaky(values):
    return jnp.maximum(values, 0.1 * values)


def tap_weights(params, grid):
    sy, sx, qy, qx = (params[n] for n in range(4))
    rows = grid[0] + grid[1] * (lax.broadcasted_iota(jnp.int32, (EXT, W), 0) - R)
    cols = lax.broadcasted_iota(jnp.int32, (EXT, W), 1)
    out = []
    across = []
    for dx in range(-R, R + 1):
        u = jnp.where(sx == dx, 1.0 - qx, jnp.where(sx == dx - 1, qx, 0.0))
        across.append(jnp.where((cols + dx >= 0) & (cols + dx < W), u, 0.0))
    for dy in range(-R, R + 1):
        v = jnp.where(sy == dy, 1.0 - qy, jnp.where(sy == dy - 1, qy, 0.0))
        at = rows + grid[1] * dy
        v = jnp.where((at >= 0) & (at < H), v, 0.0)
        for dx in range(-R, R + 1):
            w = v * across[dx + R]
            out.append(pltpu.roll(w, dx % W, 1) if dx else w)
    return out


def far_row(trio, o):
    across, own, beside = trio
    if o < 0:
        return across, (-1 - o) * C
    if o < ROWS:
        return own, o * C
    return beside, (2 * ROWS - 1 - o) * C - (ROWS * C - beside.shape[0])


def sample_row(trio, r, taps, store):
    weights = [taps(n) for n in range(25)]
    for ch in range(0, C, 16):
        g = []
        for dy in range(-R, R + 1):
            ref, at = far_row(trio, r - R + dy)
            g.append(ref[pl.ds(at + ch, 16), :])
        total = None
        for dx in range(5):
            t = g[0] * weights[dx]
            for dy in range(1, 5):
                t = t + g[dy] * weights[dy * 5 + dx]
            t = pltpu.roll(t, (R - dx) % W, 1) if dx != R else t
            total = t if total is None else total + t
        store(ch, total)


def prepare_kernel(priors, first, sense, *refs):
    refs = list(refs)
    grid = (first[0], sense[0])
    older = [refs.pop(0) for _ in range(3)] if priors == 2 else None
    params, taps = refs.pop(0), refs.pop(0)
    for n, w in enumerate(tap_weights(params[0], grid)):
        for r in range(EXT):
            taps[r, n] = jnp.broadcast_to(w[r : r + 1], (16, W)).astype(jnp.bfloat16)
    if priors < 2:
        return
    stack, wts = refs
    for n, w in enumerate(tap_weights(params[1], grid)):
        wts[n] = w
    for r in range(EXT):

        def weight(n):
            return jnp.broadcast_to(wts[n, pl.ds(r, 1), :], (16, W)).astype(jnp.bfloat16)

        def store(ch, value):
            stack[pl.ds(ch, 16), pl.ds(r * W, W)] = value

        sample_row(older, r, weight, store)


def middle_kernel(own, beside, taps, stack):
    for r in range(EARLY, EXT):

        def store(ch, value):
            stack[pl.ds(ch, 16), pl.ds((r - EARLY) * W, W)] = value

        sample_row((None, own, beside), r, lambda n: taps[r, n], store)


def step_kernel(priors, parts, first, sense, *refs):
    refs = list(refs)
    grid = (first[0], sense[0])
    sides = [[refs.pop(0) for _ in range(3)] for _ in range(parts)]
    newest = [refs.pop(0) for _ in range(2)] + [None] if priors else None
    taps = refs.pop(0) if priors else None
    middle = refs.pop(0) if priors else None
    older = refs.pop(0) if priors == 2 else None
    mixer, inner, outer, out, stack, joined, hidden = refs

    def keep(row):
        at = grid[0] + grid[1] * row
        return jnp.where((at >= 0) & (at < H), 1.0, 0.0)

    def side_row(trio, r):
        ref, at = far_row(trio, r - R)
        return ref[pl.ds(at, C), :]

    depth = (parts + priors) * C
    for r in (0, 2, 4, 6):
        for n in range(2 if priors and r < EARLY else 0):

            def store(ch, value):
                stack[pl.ds(ch, 16), pl.ds((r + n) * W, W)] = value

            sample_row(newest, r + n, lambda k: taps[r + n, k], store)
        pieces = [
            jnp.concatenate([side_row(trio, r), side_row(trio, r + 1)], axis=1) for trio in sides
        ]
        if priors:
            near = stack[:, pl.ds(r * W, 2 * W)] if r < EARLY else middle[:, pl.ds((r - EARLY) * W, 2 * W)]
            pieces.append(near)
        if priors == 2:
            pieces.append(older[:, pl.ds(r * W, 2 * W)])
        data = jnp.concatenate(pieces, axis=0)
        both = leaky(jnp.dot(mixer[:, pl.ds(0, depth)], data, preferred_element_type=jnp.float32))
        for n in range(2):
            value = both[:, n * W : (n + 1) * W]
            if not R <= r + n < R + ROWS:
                value = value * keep(r + n - R)
            joined[pl.ds((r + n) * C, C), :] = value.astype(jnp.bfloat16)

    cols = lax.broadcasted_iota(jnp.int32, (C, W), 1)

    def conv_pair(source, kernel, r):
        data = jnp.concatenate(
            [source[pl.ds(r * C, 3 * C), :], source[pl.ds((r + 1) * C, 3 * C), :]], axis=1
        )
        res = jnp.dot(kernel[...], data, preferred_element_type=jnp.float32)
        outs = []
        for n in range(2):
            part = res[:, n * W : (n + 1) * W]
            left = jnp.where(cols >= 1, pltpu.roll(part[0:C], 1, 1), 0.0)
            right = jnp.where(cols < W - 1, pltpu.roll(part[2 * C : 3 * C], W - 1, 1), 0.0)
            outs.append(left + part[C : 2 * C] + right)
        return outs

    for r in (0, 2, 4):
        for n, value in enumerate(conv_pair(joined, inner, r)):
            value = leaky(value)
            if r + n in (0, ROWS + 1):
                value = value * keep(r + n - 1)
            hidden[pl.ds((r + n) * C, C), :] = value.astype(jnp.bfloat16)

    for r in (0, 2):
        for n, value in enumerate(conv_pair(hidden, outer, r)):
            base = joined[pl.ds((r + n + R) * C, C), :].astype(jnp.float32)
            out[pl.ds((r + n) * C, C), :] = (base + value).astype(jnp.bfloat16)


def pack_kernel(sense, back_shift, back_fraction, ahead_shift, ahead_fraction, out):
    turned = sense[0] < 0
    sign = jnp.where(turned, -1.0, 1.0)
    one = jnp.where(turned, 1.0, 0.0)
    for r in range(ROWS):
        row = pl.ds(jnp.where(turned, ROWS - 1 - r, r), 1)
        rows = []
        for shift, fraction in ((back_shift, back_fraction), (ahead_shift, ahead_fraction)):
            for n in range(2):
                rows.append(shift[0, n, 0, row, :].astype(jnp.float32) * sign - one)
                rows.append(shift[0, n, 1, row, :].astype(jnp.float32))
                rows.append(fraction[0, n, 0, row, :] * sign + one)
                rows.append(fraction[0, n, 1, row, :])
        out[pl.ds(r * 16, 16), :] = jnp.concatenate(rows, axis=0).astype(BF16)


def run_prepare(grid, older, params):
    operands = list(grid) + (list(older) if older else []) + [params]
    outs = [jax.ShapeDtypeStruct((EXT, 25, 16, W), BF16)]
    if older:
        outs.append(jax.ShapeDtypeStruct((C, EXT * W), BF16))
    return pl.pallas_call(
        functools.partial(prepare_kernel, 2 if older else 1),
        out_shape=outs,
        in_specs=[SMEM, SMEM] + [VMEM] * (len(operands) - 2),
        out_specs=[VMEM] * len(outs),
        scratch_shapes=[pltpu.VMEM((25, EXT, W), jnp.float32)] if older else [],
        compiler_params=pltpu.CompilerParams(vmem_limit_bytes=16 * 2**20),
        cost_estimate=pl.CostEstimate(flops=10**10, bytes_accessed=2**20, transcendentals=0),
        name="prepare",
    )(*operands)


def run_middle(newest, taps):
    return pl.pallas_call(
        middle_kernel,
        out_shape=jax.ShapeDtypeStruct((C, (EXT - EARLY) * W), BF16),
        in_specs=[VMEM] * 3,
        out_specs=VMEM,
        compiler_params=pltpu.CompilerParams(vmem_limit_bytes=16 * 2**20),
        cost_estimate=pl.CostEstimate(flops=10**6, bytes_accessed=2**10, transcendentals=0),
        name="middle",
    )(newest[1], newest[2], taps)


def run_pack(grid, arrays):
    return pl.pallas_call(
        pack_kernel,
        out_shape=jax.ShapeDtypeStruct((ROWS * 16, W), BF16),
        in_specs=[SMEM] + [VMEM] * 4,
        out_specs=VMEM,
        compiler_params=pltpu.CompilerParams(vmem_limit_bytes=16 * 2**20),
        name="pack",
    )(grid[1], *arrays)


def run_step(grid, sides, newest, prepared, weights):
    operands = list(grid)
    for trio in sides:
        operands += list(trio)
    operands += (list(newest[:2]) if newest else []) + list(prepared) + list(weights)
    return pl.pallas_call(
        functools.partial(step_kernel, max(0, len(prepared) - 1), len(sides)),
        out_shape=jax.ShapeDtypeStruct((ROWS * C, W), BF16),
        in_specs=[SMEM, SMEM] + [VMEM] * (len(operands) - 2),
        out_specs=VMEM,
        scratch_shapes=[
            pltpu.VMEM((C, EARLY * W), BF16),
            pltpu.VMEM((EXT * C, W), BF16),
            pltpu.VMEM(((ROWS + 2) * C, W), BF16),
        ],
        compiler_params=pltpu.CompilerParams(vmem_limit_bytes=16 * 2**20),
        cost_estimate=pl.CostEstimate(flops=10**8, bytes_accessed=2**20, transcendentals=0),
        name="step",
    )(*operands)


def place(replica, low, p, count):
    x, z, core = p // 16, p // 2 % 8, p % 2
    half = z // 4
    level = 7 - z if half else z
    level = level if low else 7 - level
    return (2 * replica + half) * count + x * 16 + level * 2 + core


def mirror(q):
    return q // 16 * 16 + (7 - q // 2 % 8) * 2 + q % 2


def swap(for_across, for_beside):
    count = lax.axis_size("tile")
    across, beside = [], []
    for replica in range(4):
        for low in (True, False):
            at = [place(replica, low, p, count) for p in range(count)]
            for p in range(count):
                beside.append((at[p], at[p ^ 1]))
                other = p + 1 if p % 2 else p - 1
                if 0 <= other < count:
                    across.append((at[p], at[other]))
    axes = ("tm", "tile")
    return lax.ppermute(for_across, axes, across), lax.ppermute(for_beside, axes, beside)


def conv_matrix(kernel, odd):
    taps = kernel.reshape(C, 3, 3, C)
    taps = jnp.where(odd, taps[:, ::-1], taps)
    return taps.transpose(2, 0, 1, 3).reshape(3 * C, 3 * C)


def shards(
    frames,
    back_shift,
    back_fraction,
    ahead_shift,
    ahead_fraction,
    back_mixer,
    back_inner,
    back_outer,
    ahead_mixer,
    ahead_inner,
    ahead_outer,
):
    where = lax.axis_index("tile").astype(jnp.int32)
    turn = lax.axis_index("tm").astype(jnp.int32)
    odd = where % 2 == 1
    upper = where // 2 % 8 >= 4
    home = upper == (turn % 2 == 1)
    tile = jnp.where(home, where, mirror(where))
    grid = (
        (tile * ROWS + jnp.where(odd, ROWS - 1, 0)).reshape(1),
        jnp.where(odd, -1, 1).astype(jnp.int32).reshape(1),
    )

    def oriented(values, axis):
        return jnp.where(odd, jnp.flip(values, axis), values)

    own = oriented(frames[0].transpose(1, 0, 2), 0).reshape(ROWS * C, W)

    own_params = run_pack(grid, (back_shift, back_fraction, ahead_shift, ahead_fraction))
    mine = jnp.concatenate([own, own_params], axis=0)
    other = lax.ppermute(mine, "tile", [(q, mirror(q)) for q in range(lax.axis_size("tile"))])
    for_even = jnp.where(upper, other, mine)
    for_odd = jnp.where(upper, mine, other)
    clip = lax.all_to_all(
        jnp.broadcast_to(jnp.stack([for_even, for_odd])[None], (FRAMES // 2, 2) + mine.shape).reshape(
            (FRAMES,) + mine.shape
        ),
        "tm",
        split_axis=0,
        concat_axis=0,
    )

    top = jnp.concatenate([clip[:, : 2 * C], clip[:, 4 * C : 4 * C + 32]], axis=1)
    low = jnp.concatenate([clip[:, 2 * C : 4 * C], clip[:, 4 * C + 32 :]], axis=1)
    across, beside = swap(top, low)

    def turned(halo):
        rows = halo[:, 2 * C :].reshape(FRAMES, 2, 2, 2, 4, W)[:, ::-1].astype(jnp.float32)
        return jnp.stack([-1.0 - rows[..., 0, :], rows[..., 1, :], 1.0 - rows[..., 2, :], rows[..., 3, :]], axis=4)

    mid = clip[:, 4 * C :].reshape(FRAMES, ROWS, 2, 2, 4, W).astype(jnp.float32)
    params = jnp.concatenate([turned(across), mid, turned(beside)], axis=1).transpose(2, 0, 3, 4, 1, 5)
    frame_trios = [(across[t, : 2 * C], clip[t, : 4 * C], beside[t, : 2 * C]) for t in range(FRAMES)]

    def chain(order, way, extra, weights):
        done = {}
        history = []
        for n, t in enumerate(order):
            sides = [frame_trios[t]] + ([extra[t]] if extra else [])
            prepared = []
            if n:
                taps, *older = run_prepare(grid, history[1] if n > 1 else None, params[way, t])
                prepared = [taps, run_middle(history[0], taps)] + older
            new = run_step(grid, sides, history[0] if n else None, prepared, weights)
            if n + 1 < FRAMES or not extra:
                far, near = swap(new, new)
                done[t] = (far, new, near)
                history.insert(0, done[t])
            else:
                done[t] = (None, new, None)
        return done

    back_weights = (back_mixer, conv_matrix(back_inner, odd), conv_matrix(back_outer, odd))
    ahead_weights = (ahead_mixer, conv_matrix(ahead_inner, odd), conv_matrix(ahead_outer, odd))
    back = chain(range(FRAMES - 1, -1, -1), 0, None, back_weights)
    ahead = chain(range(FRAMES), 1, back, ahead_weights)

    def pick(done, frame):
        value = done[0][1]
        for t in range(1, FRAMES):
            value = jnp.where(frame == t, done[t][1], value)
        return value

    def results(frame):
        return jnp.stack([pick(back, frame), pick(ahead, frame)])

    count = lax.axis_size("tile")
    gives = [
        (t * count + q, (t ^ 1) * count + q)
        for t in range(FRAMES)
        for q in range(count)
        if (q // 2 % 8 >= 4) == (t % 2 == 1)
    ]
    given = lax.ppermute(results(turn ^ 1), ("tm", "tile"), gives)
    final = jnp.where(home, results(turn), given).reshape(2, ROWS, C, W)
    final = oriented(final, 1).transpose(0, 2, 1, 3)
    return final[0][None], final[1][None]


def solution(mesh):
    in_specs = (
        P("tm", None, "tile", None),
        P("tm", None, None, "tile", None),
        P("tm", None, None, "tile", None),
        P("tm", None, None, "tile", None),
        P("tm", None, None, "tile", None),
        P(),
        P(),
        P(),
        P(),
        P(),
        P(),
    )
    out_specs = (P("tm", None, "tile", None), P("tm", None, "tile", None))
    return jax.shard_map(shards, mesh=mesh, in_specs=in_specs, out_specs=out_specs, check_vma=False)
```

```python
import functools

import jax
import jax.numpy as jnp
from jax import lax
from jax.experimental import pallas as pl
from jax.experimental.pallas import tpu as pltpu
from jax.sharding import PartitionSpec as P

R = 2
C = 64
W = 128
ROWS = 4
H = 256
FRAMES = 8
EXT = ROWS + 2 * R
EARLY = EXT // 2


VMEM = pl.BlockSpec(memory_space=pltpu.VMEM)
SMEM = pl.BlockSpec(memory_space=pltpu.SMEM)
BF16 = jnp.bfloat16


def leaky(values):
    return jnp.maximum(values, 0.1 * values)


def tap_weights(params, grid):
    sy, sx, qy, qx = (params[n] for n in range(4))
    rows = grid[0] + grid[1] * (lax.broadcasted_iota(jnp.int32, (EXT, W), 0) - R)
    cols = lax.broadcasted_iota(jnp.int32, (EXT, W), 1)
    out = []
    across = []
    for dx in range(-R, R + 1):
        u = jnp.where(sx == dx, 1.0 - qx, jnp.where(sx == dx - 1, qx, 0.0))
        across.append(jnp.where((cols + dx >= 0) & (cols + dx < W), u, 0.0))
    for dy in range(-R, R + 1):
        v = jnp.where(sy == dy, 1.0 - qy, jnp.where(sy == dy - 1, qy, 0.0))
        at = rows + grid[1] * dy
        v = jnp.where((at >= 0) & (at < H), v, 0.0)
        for dx in range(-R, R + 1):
            w = v * across[dx + R]
            out.append(pltpu.roll(w, dx % W, 1) if dx else w)
    return out


def far_row(trio, o):
    across, own, beside = trio
    if o < 0:
        return across, (-1 - o) * C
    if o < ROWS:
        return own, o * C
    return beside, (2 * ROWS - 1 - o) * C - (ROWS * C - beside.shape[0])


def sample_row(trio, r, taps, store):
    weights = [taps(n) for n in range(25)]
    for ch in range(0, C, 16):
        g = []
        for dy in range(-R, R + 1):
            ref, at = far_row(trio, r - R + dy)
            g.append(ref[pl.ds(at + ch, 16), :])
        total = None
        for dx in range(5):
            t = g[0] * weights[dx]
            for dy in range(1, 5):
                t = t + g[dy] * weights[dy * 5 + dx]
            t = pltpu.roll(t, (R - dx) % W, 1) if dx != R else t
            total = t if total is None else total + t
        store(ch, total)


def prepare_kernel(priors, first, sense, *refs):
    refs = list(refs)
    grid = (first[0], sense[0])
    older = [refs.pop(0) for _ in range(3)] if priors == 2 else None
    params, taps = refs.pop(0), refs.pop(0)
    for n, w in enumerate(tap_weights(params[0], grid)):
        for r in range(EXT):
            taps[r, n] = jnp.broadcast_to(w[r : r + 1], (16, W)).astype(jnp.bfloat16)
    if priors < 2:
        return
    stack, wts = refs
    for n, w in enumerate(tap_weights(params[1], grid)):
        wts[n] = w
    for r in range(EXT):

        def weight(n):
            return jnp.broadcast_to(wts[n, pl.ds(r, 1), :], (16, W)).astype(jnp.bfloat16)

        def store(ch, value):
            stack[pl.ds(ch, 16), pl.ds(r * W, W)] = value

        sample_row(older, r, weight, store)


def block_parts(grid, sides, mixer, inner, joined, hidden, sampled):
    cols = lax.broadcasted_iota(jnp.int32, (C, W), 1)

    def keep(row):
        at = grid[0] + grid[1] * row
        return jnp.where((at >= 0) & (at < H), 1.0, 0.0)

    def side_row(trio, r):
        ref, at = far_row(trio, r - R)
        return ref[pl.ds(at, C), :]

    def join(r):
        pieces = [
            jnp.concatenate([side_row(trio, r), side_row(trio, r + 1)], axis=1) for trio in sides
        ] + sampled(r)
        data = jnp.concatenate(pieces, axis=0)
        weights = mixer[:, pl.ds(0, data.shape[0])]
        both = leaky(jnp.dot(weights, data, preferred_element_type=jnp.float32))
        for n in range(2):
            value = both[:, n * W : (n + 1) * W]
            if not R <= r + n < R + ROWS:
                value = value * keep(r + n - R)
            joined[pl.ds((r + n) * C, C), :] = value.astype(BF16)

    def conv_pair(source, kernel, r):
        data = jnp.concatenate(
            [source[pl.ds(r * C, 3 * C), :], source[pl.ds((r + 1) * C, 3 * C), :]], axis=1
        )
        res = jnp.dot(kernel[...], data, preferred_element_type=jnp.float32)
        outs = []
        for n in range(2):
            part = res[:, n * W : (n + 1) * W]
            left = jnp.where(cols >= 1, pltpu.roll(part[0:C], 1, 1), 0.0)
            right = jnp.where(cols < W - 1, pltpu.roll(part[2 * C : 3 * C], W - 1, 1), 0.0)
            outs.append(left + part[C : 2 * C] + right)
        return outs

    def inside(r):
        for n, value in enumerate(conv_pair(joined, inner, r)):
            value = leaky(value)
            if r + n in (0, ROWS + 1):
                value = value * keep(r + n - 1)
            hidden[pl.ds((r + n) * C, C), :] = value.astype(BF16)

    return join, inside, conv_pair


def middle_kernel(priors, parts, first, sense, *refs):
    refs = list(refs)
    grid = (first[0], sense[0])
    sides = [[None] + [refs.pop(0) for _ in range(2)] for _ in range(parts)]
    own, beside, taps = (refs.pop(0) for _ in range(3))
    older = refs.pop(0) if priors == 2 else None
    mixer, inner, joined_out, hidden_out, stack, joined, hidden = refs
    for r in range(EARLY, EXT):

        def store(ch, value):
            stack[pl.ds(ch, 16), pl.ds((r - EARLY) * W, W)] = value

        sample_row((None, own, beside), r, lambda n: taps[r, n], store)

    def sampled(r):
        near = [stack[:, pl.ds((r - EARLY) * W, 2 * W)]]
        return near + ([older[:, pl.ds(r * W, 2 * W)]] if older is not None else [])

    join, inside, _ = block_parts(grid, sides, mixer, inner, joined, hidden, sampled)
    join(4)
    join(6)
    inside(4)
    joined_out[...] = joined[pl.ds(EARLY * C, (EXT - EARLY) * C), :]
    hidden_out[...] = hidden[pl.ds(ROWS * C, 2 * C), :]


def step_kernel(priors, parts, first, sense, *refs):
    refs = list(refs)
    grid = (first[0], sense[0])
    sides = [[refs.pop(0) for _ in range(3)] for _ in range(parts)]
    newest = [refs.pop(0) for _ in range(2)] + [None] if priors else None
    taps = refs.pop(0) if priors else None
    ready = [refs.pop(0) for _ in range(2)] if priors else None
    older = refs.pop(0) if priors == 2 else None
    mixer, inner, outer, out, stack, joined, hidden = refs

    def sampled(r):
        near = [stack[:, pl.ds(r * W, 2 * W)]] if priors else []
        return near + ([older[:, pl.ds(r * W, 2 * W)]] if older is not None else [])

    join, inside, conv_pair = block_parts(grid, sides, mixer, inner, joined, hidden, sampled)
    if priors:
        joined[pl.ds(EARLY * C, (EXT - EARLY) * C), :] = ready[0][...]
        hidden[pl.ds(ROWS * C, 2 * C), :] = ready[1][...]
    for r in (0, 2) if priors else (0, 2, 4, 6):
        for n in range(2 if priors else 0):

            def store(ch, value):
                stack[pl.ds(ch, 16), pl.ds((r + n) * W, W)] = value

            sample_row(newest, r + n, lambda k: taps[r + n, k], store)
        join(r)
    for r in (0, 2) if priors else (0, 2, 4):
        inside(r)
    for r in (0, 2):
        for n, value in enumerate(conv_pair(hidden, outer, r)):
            base = joined[pl.ds((r + n + R) * C, C), :].astype(jnp.float32)
            out[pl.ds((r + n) * C, C), :] = (base + value).astype(BF16)


def pack_kernel(sense, back_shift, back_fraction, ahead_shift, ahead_fraction, out):
    turned = sense[0] < 0
    sign = jnp.where(turned, -1.0, 1.0)
    one = jnp.where(turned, 1.0, 0.0)
    for r in range(ROWS):
        row = pl.ds(jnp.where(turned, ROWS - 1 - r, r), 1)
        rows = []
        for shift, fraction in ((back_shift, back_fraction), (ahead_shift, ahead_fraction)):
            for n in range(2):
                rows.append(shift[0, n, 0, row, :].astype(jnp.float32) * sign - one)
                rows.append(shift[0, n, 1, row, :].astype(jnp.float32))
                rows.append(fraction[0, n, 0, row, :] * sign + one)
                rows.append(fraction[0, n, 1, row, :])
        out[pl.ds(r * 16, 16), :] = jnp.concatenate(rows, axis=0).astype(BF16)


def run_prepare(grid, older, params):
    operands = list(grid) + (list(older) if older else []) + [params]
    outs = [jax.ShapeDtypeStruct((EXT, 25, 16, W), BF16)]
    if older:
        outs.append(jax.ShapeDtypeStruct((C, EXT * W), BF16))
    return pl.pallas_call(
        functools.partial(prepare_kernel, 2 if older else 1),
        out_shape=outs,
        in_specs=[SMEM, SMEM] + [VMEM] * (len(operands) - 2),
        out_specs=[VMEM] * len(outs),
        scratch_shapes=[pltpu.VMEM((25, EXT, W), jnp.float32)] if older else [],
        compiler_params=pltpu.CompilerParams(vmem_limit_bytes=16 * 2**20),
        cost_estimate=pl.CostEstimate(flops=10**10, bytes_accessed=2**20, transcendentals=0),
        name="prepare",
    )(*operands)


def run_middle(grid, sides, newest, taps, older, weights):
    operands = list(grid)
    for trio in sides:
        operands += list(trio[1:])
    operands += list(newest[1:]) + [taps] + older + list(weights[:2])
    return pl.pallas_call(
        functools.partial(middle_kernel, 1 + len(older), len(sides)),
        out_shape=[
            jax.ShapeDtypeStruct(((EXT - EARLY) * C, W), BF16),
            jax.ShapeDtypeStruct((2 * C, W), BF16),
        ],
        in_specs=[SMEM, SMEM] + [VMEM] * (len(operands) - 2),
        out_specs=[VMEM] * 2,
        scratch_shapes=[
            pltpu.VMEM((C, (EXT - EARLY) * W), BF16),
            pltpu.VMEM((EXT * C, W), BF16),
            pltpu.VMEM(((ROWS + 2) * C, W), BF16),
        ],
        compiler_params=pltpu.CompilerParams(vmem_limit_bytes=16 * 2**20),
        cost_estimate=pl.CostEstimate(flops=10**6, bytes_accessed=2**10, transcendentals=0),
        name="middle",
    )(*operands)


def run_pack(grid, arrays):
    return pl.pallas_call(
        pack_kernel,
        out_shape=jax.ShapeDtypeStruct((ROWS * 16, W), BF16),
        in_specs=[SMEM] + [VMEM] * 4,
        out_specs=VMEM,
        compiler_params=pltpu.CompilerParams(vmem_limit_bytes=16 * 2**20),
        name="pack",
    )(grid[1], *arrays)


def run_step(grid, sides, newest, prepared, weights):
    operands = list(grid)
    for trio in sides:
        operands += list(trio)
    operands += (list(newest[:2]) if newest else []) + list(prepared) + list(weights)
    return pl.pallas_call(
        functools.partial(step_kernel, max(0, len(prepared) - 2), len(sides)),
        out_shape=jax.ShapeDtypeStruct((ROWS * C, W), BF16),
        in_specs=[SMEM, SMEM] + [VMEM] * (len(operands) - 2),
        out_specs=VMEM,
        scratch_shapes=[
            pltpu.VMEM((C, EARLY * W), BF16),
            pltpu.VMEM((EXT * C, W), BF16),
            pltpu.VMEM(((ROWS + 2) * C, W), BF16),
        ],
        compiler_params=pltpu.CompilerParams(vmem_limit_bytes=16 * 2**20),
        cost_estimate=pl.CostEstimate(flops=10**8, bytes_accessed=2**20, transcendentals=0),
        name="step",
    )(*operands)


def place(replica, low, p, count):
    x, z, core = p // 16, p // 2 % 8, p % 2
    half = z // 4
    level = 7 - z if half else z
    level = level if low else 7 - level
    return (2 * replica + half) * count + x * 16 + level * 2 + core


def mirror(q):
    return q // 16 * 16 + (7 - q // 2 % 8) * 2 + q % 2


def swap(for_across, for_beside):
    count = lax.axis_size("tile")
    across, beside = [], []
    for replica in range(4):
        for low in (True, False):
            at = [place(replica, low, p, count) for p in range(count)]
            for p in range(count):
                beside.append((at[p], at[p ^ 1]))
                other = p + 1 if p % 2 else p - 1
                if 0 <= other < count:
                    across.append((at[p], at[other]))
    axes = ("tm", "tile")
    return lax.ppermute(for_across, axes, across), lax.ppermute(for_beside, axes, beside)


def conv_matrix(kernel, odd):
    taps = kernel.reshape(C, 3, 3, C)
    taps = jnp.where(odd, taps[:, ::-1], taps)
    return taps.transpose(2, 0, 1, 3).reshape(3 * C, 3 * C)


def shards(
    frames,
    back_shift,
    back_fraction,
    ahead_shift,
    ahead_fraction,
    back_mixer,
    back_inner,
    back_outer,
    ahead_mixer,
    ahead_inner,
    ahead_outer,
):
    where = lax.axis_index("tile").astype(jnp.int32)
    turn = lax.axis_index("tm").astype(jnp.int32)
    odd = where % 2 == 1
    upper = where // 2 % 8 >= 4
    home = upper == (turn % 2 == 1)
    tile = jnp.where(home, where, mirror(where))
    grid = (
        (tile * ROWS + jnp.where(odd, ROWS - 1, 0)).reshape(1),
        jnp.where(odd, -1, 1).astype(jnp.int32).reshape(1),
    )

    def oriented(values, axis):
        return jnp.where(odd, jnp.flip(values, axis), values)

    own = oriented(frames[0].transpose(1, 0, 2), 0).reshape(ROWS * C, W)

    own_params = run_pack(grid, (back_shift, back_fraction, ahead_shift, ahead_fraction))
    mine = jnp.concatenate([own, own_params], axis=0)
    other = lax.ppermute(mine, "tile", [(q, mirror(q)) for q in range(lax.axis_size("tile"))])
    for_even = jnp.where(upper, other, mine)
    for_odd = jnp.where(upper, mine, other)
    clip = lax.all_to_all(
        jnp.broadcast_to(jnp.stack([for_even, for_odd])[None], (FRAMES // 2, 2) + mine.shape).reshape(
            (FRAMES,) + mine.shape
        ),
        "tm",
        split_axis=0,
        concat_axis=0,
    )

    top = jnp.concatenate([clip[:, : 2 * C], clip[:, 4 * C : 4 * C + 32]], axis=1)
    low = jnp.concatenate([clip[:, 2 * C : 4 * C], clip[:, 4 * C + 32 :]], axis=1)
    across, beside = swap(top, low)

    def turned(halo):
        rows = halo[:, 2 * C :].reshape(FRAMES, 2, 2, 2, 4, W)[:, ::-1].astype(jnp.float32)
        return jnp.stack([-1.0 - rows[..., 0, :], rows[..., 1, :], 1.0 - rows[..., 2, :], rows[..., 3, :]], axis=4)

    mid = clip[:, 4 * C :].reshape(FRAMES, ROWS, 2, 2, 4, W).astype(jnp.float32)
    params = jnp.concatenate([turned(across), mid, turned(beside)], axis=1).transpose(2, 0, 3, 4, 1, 5)
    frame_trios = [(across[t, : 2 * C], clip[t, : 4 * C], beside[t, : 2 * C]) for t in range(FRAMES)]

    def chain(order, way, extra, weights):
        done = {}
        history = []
        for n, t in enumerate(order):
            sides = [frame_trios[t]] + ([extra[t]] if extra else [])
            prepared = []
            if n:
                taps, *older = run_prepare(grid, history[1] if n > 1 else None, params[way, t])
                prepared = [taps, *run_middle(grid, sides, history[0], taps, older, weights)] + older
            new = run_step(grid, sides, history[0] if n else None, prepared, weights)
            if n + 1 < FRAMES or not extra:
                far, near = swap(new, new)
                done[t] = (far, new, near)
                history.insert(0, done[t])
            else:
                done[t] = (None, new, None)
        return done

    back_weights = (back_mixer, conv_matrix(back_inner, odd), conv_matrix(back_outer, odd))
    ahead_weights = (ahead_mixer, conv_matrix(ahead_inner, odd), conv_matrix(ahead_outer, odd))
    back = chain(range(FRAMES - 1, -1, -1), 0, None, back_weights)
    ahead = chain(range(FRAMES), 1, back, ahead_weights)

    def pick(done, frame):
        value = done[0][1]
        for t in range(1, FRAMES):
            value = jnp.where(frame == t, done[t][1], value)
        return value

    def results(frame):
        return jnp.stack([pick(back, frame), pick(ahead, frame)])

    count = lax.axis_size("tile")
    gives = [
        (t * count + q, (t ^ 1) * count + q)
        for t in range(FRAMES)
        for q in range(count)
        if (q // 2 % 8 >= 4) == (t % 2 == 1)
    ]
    given = lax.ppermute(results(turn ^ 1), ("tm", "tile"), gives)
    final = jnp.where(home, results(turn), given).reshape(2, ROWS, C, W)
    final = oriented(final, 1).transpose(0, 2, 1, 3)
    return final[0][None], final[1][None]


def solution(mesh):
    in_specs = (
        P("tm", None, "tile", None),
        P("tm", None, None, "tile", None),
        P("tm", None, None, "tile", None),
        P("tm", None, None, "tile", None),
        P("tm", None, None, "tile", None),
        P(),
        P(),
        P(),
        P(),
        P(),
        P(),
    )
    out_specs = (P("tm", None, "tile", None), P("tm", None, "tile", None))
    return jax.shard_map(shards, mesh=mesh, in_specs=in_specs, out_specs=out_specs, check_vma=False)
```
